512 devices in a mesh: seq: 32 (over y, z_hi, core), chan: 16 (over x, z_lo).
Axes of the slice: x: 4, y: 4, z: 16 (z_hi: 4, z_lo: 4; z = z_hi * 4 + z_lo), core: 2. Of those that a mesh axis runs over, the one named last changes fastest.
Arguments:
- frames: bfloat16 [10, 1536, 16384], P(None, 'chan', 'seq'), may hold values from -6 to 6
- conv_taps: float32 [4, 1536], P(None, 'chan'), may hold values from -3 to 3
- left_factor: bfloat16 [32, 512, 512], P('seq'), may hold values from -0.25 to 0.25
- right_factor: bfloat16 [512, 32, 32], P('seq'), may hold values from -1 to 1
- out_grad: bfloat16 [10, 1536, 16384], P(None, 'chan', 'seq'), may hold values from -6 to 6
Outputs:
- mixed: bfloat16 [10, 1536, 16384], P(None, 'chan', 'seq')
- frames_grad: bfloat16 [10, 1536, 16384], P(None, 'chan', 'seq')
- left_grad: float32 [32, 512, 512], P('seq', 'chan')
- right_grad: float32 [512, 32, 32], P('seq', 'chan')
The draws below stay inside these ranges and needn't reach their ends.
All inputs are finite; a program needn't handle non-finite values.
Results may differ from the reference program's by a relative error of at most 0.0057.
Values may be sent and summed in bfloat16 or wider, within the bound.
No kernel may reach another device: no remote copies, remote signals or barrier semaphores. Data moves between devices by JAX's collectives and lax.ppermute only.
A program may use at most 64 MiB of HBM per device.

```python
from functools import partial
import jax
import jax.numpy as jnp
from jax import lax

D = 1536
BLK = 512
TAPS = 4
CLIPS = 10
NBLK = 32
L = 16384


def steps_of(own_key, shape, split, least, largest):
    def one(axis_at, parts):
        heights = jax.random.uniform(jax.random.fold_in(jax.random.fold_in(own_key, 6), axis_at), (parts,), jnp.float32, least / len(split), largest / len(split))
        return jnp.repeat(jnp.exp(heights), shape[axis_at] // parts).reshape((-1,) + (1,) * (len(shape) - axis_at - 1))

    level = one(*split[0])
    for cut in split[1:]:
        level = level * one(*cut)
    return level


def centred(key, extent, scale, reach, cuts=(), held_as=jnp.bfloat16):
    drawn = scale * jax.random.normal(key, extent, jnp.float32)
    if cuts:
        drawn = drawn * steps_of(key, extent, cuts, -0.22, 0.18)
    return jnp.clip(drawn, -reach, reach).astype(held_as)


def setup_inputs(seed: int = 0) -> dict:
    key_list = jax.random.split(jax.random.key(seed), 6)
    return {
        "frames": centred(key_list[0], (CLIPS, D, L), 1.0, 6.0, ((1, 16), (2, 32))),
        "conv_taps": centred(key_list[1], (TAPS, D), 0.5, 3.0, ((1, 16),), jnp.float32),
        "left_factor": centred(key_list[2], (NBLK, BLK, BLK), BLK ** -0.5, 0.25, ((0, 32),)),
        "right_factor": centred(key_list[3], (BLK, NBLK, NBLK), NBLK ** -0.5, 1.0, ((0, 32),)),
        "out_grad": centred(key_list[4], (CLIPS, D, L), 1.0, 6.0, ((1, 16), (2, 32))),
    }


def clip_pass(left_w, right_w, taps, carry, pair):
    clip, cot = pair
    left_sum, right_sum = carry
    xf = clip.astype(jnp.float32)
    padded = jnp.pad(xf, ((0, 0), (TAPS - 1, 0)))
    mixed_conv = jnp.zeros((D, L), jnp.float32)
    for step in range(TAPS):
        mixed_conv = mixed_conv + taps[step][:, None] * padded[:, TAPS - 1 - step:TAPS - 1 - step + L]
    conv = mixed_conv.astype(jnp.bfloat16)
    blocks = conv.astype(jnp.float32).reshape(D, NBLK, BLK)
    first = jnp.einsum('dij,ijk->dik', blocks, left_w.astype(jnp.float32)).astype(jnp.bfloat16)
    firstf = first.astype(jnp.float32)
    second = jnp.einsum('dik,kim->dkm', firstf, right_w.astype(jnp.float32)).reshape(D, L)
    sig = jax.nn.sigmoid(xf)
    gate = xf * sig
    output = (second * gate).astype(jnp.bfloat16)
    cotf = cot.astype(jnp.float32)
    dsecond = (cotf * gate).astype(jnp.bfloat16)
    gate_part = cotf * second * sig * (1.0 + xf * (1.0 - sig))
    dsb = dsecond.astype(jnp.float32).reshape(D, BLK, NBLK)
    right_part = jnp.einsum('dik,dkm->kim', firstf, dsb)
    dfirst = jnp.einsum('dkm,kim->dik', dsb, right_w.astype(jnp.float32)).astype(jnp.bfloat16)
    dff = dfirst.astype(jnp.float32)
    left_part = jnp.einsum('dij,dik->ijk', blocks, dff)
    dconv = jnp.einsum('dik,ijk->dij', dff, left_w.astype(jnp.float32)).reshape(D, L)
    padded_back = jnp.pad(dconv, ((0, 0), (0, TAPS - 1)))
    conv_back = jnp.zeros((D, L), jnp.float32)
    for step in range(TAPS):
        conv_back = conv_back + taps[step][:, None] * padded_back[:, step:step + L]
    grad_out = (gate_part + conv_back).astype(jnp.bfloat16)
    return (left_sum + left_part, right_sum + right_part), (output, grad_out)


def reference(frames, conv_taps, left_factor, right_factor, out_grad):
    stepper = partial(clip_pass, left_factor, right_factor, conv_taps.astype(jnp.float32))
    start = (jnp.zeros((NBLK, BLK, BLK), jnp.float32), jnp.zeros((BLK, NBLK, NBLK), jnp.float32))
    sums, outs = lax.scan(stepper, start, (frames, out_grad))
    return outs[0], outs[1], sums[0], sums[1]
```

```python
import functools

import jax
import jax.numpy as jnp
from jax import lax
from jax.experimental import pallas as pl
from jax.experimental.pallas import tpu as pltpu
from jax.sharding import Mesh
from jax.sharding import PartitionSpec as P

TAPS = 4
CLIPS = 10
LANES = 128
SEQ = ("y", "zh", "c")
CHAN = ("x", "zl")
F32 = jnp.float32
BF16 = jnp.bfloat16
HIGHEST = lax.Precision.HIGHEST
LIMIT = pltpu.CompilerParams(vmem_limit_bytes=24 * 1024 * 1024)


def dot(left, right, sides, precision=None):
    return lax.dot_general(
        left,
        right,
        (((sides[0],), (sides[1],)), ((), ())),
        precision=precision,
        preferred_element_type=F32,
    )


def iota(shape, axis):
    return lax.broadcasted_iota(jnp.int32, shape, axis)


def call(kernel, outs, scratch=(), flops=1 << 29, moved=1 << 22, scalars=0, arrays=0):
    specs = {}
    if scalars:
        specs["in_specs"] = [pl.BlockSpec(memory_space=pltpu.SMEM)] * scalars + [
            pl.BlockSpec(memory_space=pltpu.VMEM)
        ] * arrays
    return pl.pallas_call(
        kernel,
        **specs,
        out_shape=[jax.ShapeDtypeStruct(shape, dtype) for shape, dtype in outs],
        scratch_shapes=list(scratch),
        compiler_params=LIMIT,
        cost_estimate=pl.CostEstimate(flops=flops, bytes_accessed=moved, transcendentals=0),
    )


def put_blocks(out_refs, at, rows, piece):
    blocks = piece.astype(BF16).reshape(32, rows, LANES)
    each = 32 // len(out_refs)
    for part, out_ref in enumerate(out_refs):
        out_ref[:, pl.ds(at, rows), :] = blocks[part * each : (part + 1) * each]


def put_tiles(out_refs, at, value):
    for tile in range(value.shape[1] // LANES):
        put_blocks(out_refs, (at + tile) * 16, 16, value[:, tile * LANES : (tile + 1) * LANES])


def halves(matrix):
    parts = matrix.reshape(32, 16, matrix.shape[1])
    return [parts[:, low : low + 8].reshape(256, -1).astype(BF16) for low in (0, 8)]


def put_rest(out_refs, matrix, rest):
    low, high = halves(matrix)
    none = jnp.zeros_like(rest)
    packed = dot(low, jnp.concatenate([rest, none], 0), (1, 1)) + dot(
        high, jnp.concatenate([none, rest], 0), (1, 1)
    )
    put_blocks(out_refs, 112, 8, packed)


def get_tiles(in_ref, held_ref):
    for tile in range(7):
        held_ref[:, tile * LANES : (tile + 1) * LANES] = in_ref[:, pl.ds(tile * 16, 16), :].reshape(512, LANES)
    rest = in_ref[:, pl.ds(112, 8), :].astype(F32)
    first = iota(rest.shape, 2) < 64
    low = jnp.where(first, rest, 0.0)
    high = jnp.where(first, pltpu.roll(rest, 64, 2), 0.0)
    whole = jnp.concatenate([low, high], 1).reshape(512, LANES)
    held_ref[:, 7 * LANES :] = whole.astype(BF16)


def owner(place_ref, y, zh, c):
    return (
        lax.rem(place_ref[0] + y, 4) * 8 + lax.rem(place_ref[1] + zh, 4) * 2 + lax.rem(place_ref[2] + c, 2)
    )


def edge_kernel(frames_ref, edge_ref):
    pick = (iota((16, LANES), 1) == iota((16, LANES), 0) + 112).astype(BF16)
    edge_ref[...] = dot(pick, frames_ref[:, 384:], (1, 1)).astype(BF16)


def widened(right_ref):
    row, column = iota((512, 512), 0), iota((512, 512), 1)
    order = (column == (row % 16) * 32 + row // 16).astype(BF16)
    repeat = (iota((32, 512), 0) == iota((32, 512), 1) % 32).astype(BF16)
    tall = dot(order, right_ref[...], (1, 0)).astype(BF16)
    return jnp.where(column // 32 == row % 16, dot(tall, repeat, (1, 0)), 0.0)


def gated(frames_ref, grad_ref, here):
    x = frames_ref[here, :].astype(F32)
    cot = grad_ref[here, :].astype(F32)
    return (cot * (x * jax.nn.sigmoid(x))).astype(BF16)


def back_kernel(frames_ref, grad_ref, right_ref, out_ref):
    wide = widened(right_ref)
    narrow = wide.astype(BF16)
    for at in range(0, 960, 256):
        rows = min(256, 960 - at)
        dsecond = gated(frames_ref, grad_ref, pl.ds(at, rows))
        whole = rows // LANES * LANES
        put_tiles([out_ref], at // LANES, dot(narrow, dsecond[:whole], (1, 1)))
        if rows > whole:
            put_rest([out_ref], wide, dsecond[whole:])


def gate_kernel(frames_ref, grad_ref, right_ref, dsecond_ref, wide_ref):
    wide_ref[...] = widened(right_ref).astype(BF16)
    dsecond_ref[960:, :] = jnp.zeros((64, 512), BF16)
    for at in range(0, 960, 192):
        here = pl.ds(at, 192)
        dsecond_ref[here, :] = gated(frames_ref, grad_ref, here)


def conv_kernel(place_ref, frames_ref, edge_ref, taps_ref, left_ref, conv_ref, near_ref, far_ref, turned_ref, order_ref):
    place = (iota((16, LANES), 1) == iota((16, LANES), 0) + 112).astype(BF16)
    lane = iota((96, LANES), 1)
    for clip in range(CLIPS):
        here = pl.ds(clip * 96, 96)
        x = frames_ref[here, :].astype(F32)
        before = dot(edge_ref[:, clip * 96 : (clip + 1) * 96], place, (0, 0))
        total = taps_ref[:, 0:1] * x
        for step in range(1, TAPS):
            moved = pltpu.roll(x, step, 1)
            start = jnp.where(lane < step, pltpu.roll(before, step, 1), moved[:, :LANES])
            total = total + taps_ref[:, step : step + 1] * jnp.concatenate([start, moved[:, LANES:]], 1)
        conv_ref[here, :] = total.astype(BF16)
    conv_ref[960:, :] = jnp.zeros((64, 512), BF16)
    turned_ref[...] = left_ref[...].astype(F32).T.reshape(32, 16, 512)
    for block in range(32):
        order_ref[block] = turned_ref[owner(place_ref, block // 4 % 4, block % 4, block // 16)]
    turned = order_ref[...].reshape(512, 512)
    narrow = turned.astype(BF16)
    for at in range(0, 960, 256):
        rows = min(256, 960 - at)
        whole = rows // LANES * LANES
        conv = conv_ref[pl.ds(at, rows), :]
        put_tiles([near_ref, far_ref], at // LANES, dot(narrow, conv[:whole], (1, 1)))
        if rows > whole:
            put_rest([near_ref, far_ref], turned, conv[whole:])


def left_kernel(in_ref, conv_ref, left_ref, part_ref, dfirst_ref, edge_ref):
    get_tiles(in_ref, dfirst_ref)
    edge_ref[...] = dot(left_ref[0:16, :], dfirst_ref[...], (1, 0))[0:8]
    part_ref[...] = dot(conv_ref[...], dfirst_ref[...], (0, 1))


def dconv_kernel(dfirst_ref, taps_ref, left_ref, back_ref):
    dconv = dot(dfirst_ref[...], left_ref[...], (0, 1))
    lane = iota((96, LANES), 1)
    for clip in range(CLIPS):
        y = dconv[clip * 96 : (clip + 1) * 96]
        total = taps_ref[:, 0:1] * y
        for step in range(1, TAPS):
            moved = pltpu.roll(y, 512 - step, 1)
            end = jnp.where(lane < LANES - step, moved[:, 384:], 0.0)
            total = total + taps_ref[:, step : step + 1] * jnp.concatenate([moved[:, :384], end], 1)
        back_ref[pl.ds(clip * 96, 96), :] = total


def right_kernel(place_ref, in0_ref, in1_ref, in2_ref, in3_ref, dsecond_ref, part_ref, first_ref):
    for zh, in_ref in enumerate((in0_ref, in1_ref, in2_ref, in3_ref)):
        rest = in_ref[:, pl.ds(112, 8), :].astype(F32)
        begin = iota(rest.shape, 2) < 64
        low = jnp.where(begin, rest, 0.0)
        high = jnp.where(begin, pltpu.roll(rest, 64, 2), 0.0)
        last = jnp.concatenate([low, high], 1).astype(BF16)
        for block in range(8):
            source = owner(place_ref, 4 - block // 2, 4 - zh, 2 - block % 2)
            for tile in range(7):
                first_ref[source, :, tile * LANES : (tile + 1) * LANES] = in_ref[block, pl.ds(tile * 16, 16), :]
            first_ref[source, :, 7 * LANES :] = last[block]
    for at in range(0, 512, 128):
        full = dot(first_ref[pl.ds(at // 16, 8)].reshape(128, 1024), dsecond_ref[...], (1, 0))
        kept = jnp.where(iota(full.shape, 1) // 32 == iota(full.shape, 0) % 16, full, 0.0)
        total = jnp.sum(kept.reshape(8, 16, 512), 1)
        for tile in range(4):
            part_ref[pl.ds(at // 4 + tile, 8, stride=4), :] = total[:, tile * LANES : (tile + 1) * LANES]


def end_kernel(first_ref, wide_ref, frames_ref, grad_ref, back_ref, after_ref, taps_ref, mixed_ref, out_ref):
    place = (iota((8, LANES), 1) == iota((8, LANES), 0)).astype(F32)
    lane = iota((96, LANES), 1)
    second = dot(first_ref[...].reshape(512, 1024), wide_ref[...], (0, 0))
    for clip in range(CLIPS):
        here = pl.ds(clip * 96, 96)
        x = frames_ref[here, :].astype(F32)
        cot = grad_ref[here, :].astype(F32)
        sig = jax.nn.sigmoid(x)
        sec = second[clip * 96 : (clip + 1) * 96]
        mixed_ref[here, :] = (sec * (x * sig)).astype(BF16)
        total = cot * sec * sig * (1.0 + x * (1.0 - sig)) + back_ref[here, :]
        after = dot(after_ref[:, clip * 96 : (clip + 1) * 96], place, (0, 0), HIGHEST)
        end = total[:, 384:]
        for step in range(1, TAPS):
            term = taps_ref[:, step : step + 1] * pltpu.roll(after, LANES - step, 1)
            end = end + jnp.where(lane >= LANES - step, term, 0.0)
        out_ref[here, :] = jnp.concatenate([total[:, :384], end], 1).astype(BF16)


def exchange(value, axes):
    return lax.all_to_all(value, axes, split_axis=0, concat_axis=0, tiled=True)


def along_seq(value, steps):
    pairs = [(s, s + steps) for s in range(32) if 0 <= s + steps < 32]
    return lax.ppermute(value, SEQ, pairs)


def ahead(value, axis, step):
    count = lax.axis_size(axis)
    return lax.ppermute(value, axis, [(s, (s + step) % count) for s in range(count)])


def gather_rows(near, far):
    shape = (4, 4, 120, LANES)
    near, far = near.reshape(shape), ahead(far, "c", 1).reshape(shape)
    both = [jnp.stack([near[step], far[step]]) for step in range(4)]
    both = [both[0]] + [ahead(both[step], "y", step) for step in range(1, 4)]
    return [jnp.stack([part[:, step] for part in both]).reshape(8, 120, LANES) for step in range(4)]


def halved(part, axis, apart):
    rows = part.shape[0] // 2
    upper = lax.axis_index(axis) // apart % 2
    mine = lax.dynamic_slice_in_dim(part, upper * rows, rows, 0)
    other = lax.dynamic_slice_in_dim(part, (1 - upper) * rows, rows, 0)
    return mine + lax.ppermute(other, axis, [(s, s ^ apart) for s in range(lax.axis_size(axis))])


def summed(part, axis):
    count = lax.axis_size(axis)
    me = lax.axis_index(axis)
    rows = part.shape[0] // count

    def quarter(step):
        return lax.dynamic_slice_in_dim(part, lax.rem(me + step, count) * rows, rows, 0)

    arrived = [ahead(quarter(step), axis, step) for step in range(1, count)]
    return functools.reduce(jnp.add, arrived, quarter(0))


def total_kernel(in_ref, out_ref):
    total = jnp.sum(in_ref[...], 0)
    for row in range(8):
        for group in range(4):
            piece = total[row : row + 1, group * 32 : group * 32 + 32]
            out_ref[row % 4 * 4 + group, row // 4 : row // 4 + 1, :] = piece


def shards(frames, conv_taps, left_factor, right_factor, out_grad):
    x = frames.reshape(960, 512)
    cot = out_grad.reshape(960, 512)
    left = left_factor.reshape(512, 512)
    taps = conv_taps.T
    blocks = ((32, 120, LANES), BF16)

    (edge,) = call(edge_kernel, [((16, 960), BF16)])(x)
    edge = along_seq(edge, 1)
    right = right_factor.reshape(512, 32)
    (sent_back,) = call(back_kernel, [blocks])(x, cot, right)
    sent_back, edge = lax.optimization_barrier((sent_back, edge))
    back = exchange(sent_back, SEQ)
    place = jnp.stack([lax.axis_index(axis) for axis in SEQ]).astype(jnp.int32)
    part = ((16, 120, LANES), BF16)
    conv, near, far = call(
        conv_kernel,
        [((1024, 512), BF16), part, part],
        scratch=[pltpu.VMEM((32, 16, 512), F32)] * 2,
        scalars=1,
        arrays=4,
    )(place, x, edge, taps, left)
    rows = gather_rows(near, far)
    columns = [rows[0]] + [ahead(rows[step], "zh", step) for step in range(1, 4)]

    left_part, dfirst, dedge = call(left_kernel, [((512, 512), F32), ((512, 1024), BF16), ((8, 1024), F32)])(
        back, conv, left
    )
    after = along_seq(dedge, -1)
    left_sum = summed(left_part, "x")
    (conv_back,) = call(dconv_kernel, [((960, 512), F32)])(dfirst, taps, left)
    late = lax.optimization_barrier((x, cot, right, dedge))
    dsecond, wide = call(gate_kernel, [((1024, 512), BF16), ((512, 512), BF16)])(*late[:3])
    columns, conv_back, dsecond, wide = lax.optimization_barrier(
        (columns, conv_back, dsecond, wide)
    )
    left_grad = summed(left_sum, "zl")

    right_part, first = call(right_kernel, [((128, LANES), F32), ((32, 16, 1024), BF16)], scalars=1, arrays=5)(
        place, *columns, dsecond
    )
    right_all = exchange(right_part.reshape(16, 8, LANES), CHAN)
    mixed, frames_grad = call(end_kernel, [((960, 512), BF16), ((960, 512), BF16)])(
        first, wide, x, cot, conv_back, after, taps
    )
    (right_grad,) = call(total_kernel, [((16, 2, 32), F32)])(right_all)
    return (
        mixed.reshape(frames.shape),
        frames_grad.reshape(frames.shape),
        left_grad.reshape(1, 32, 512),
        right_grad,
    )


def solution(mesh):
    fine = Mesh(mesh.devices.reshape(4, 4, 2, 4, 4), SEQ + CHAN)
    placed = (
        P(None, CHAN, SEQ),
        P(None, CHAN),
        P(SEQ, None, None),
        P(SEQ, None, None),
        P(None, CHAN, SEQ),
    )
    return jax.shard_map(
        shards,
        mesh=fine,
        in_specs=placed,
        out_specs=(
            P(None, CHAN, SEQ),
            P(None, CHAN, SEQ),
            P(SEQ, CHAN, None),
            P(SEQ, CHAN, None),
        ),
        check_vma=False,
    )
```

```python
import functools

import jax
import jax.numpy as jnp
from jax import lax
from jax.experimental import pallas as pl
from jax.experimental.pallas import tpu as pltpu
from jax.sharding import Mesh
from jax.sharding import PartitionSpec as P

TAPS = 4
CLIPS = 10
LANES = 128
SEQ = ("y", "zh", "c")
CHAN = ("x", "zl")
F32 = jnp.float32
BF16 = jnp.bfloat16
HIGHEST = lax.Precision.HIGHEST
LIMIT = pltpu.CompilerParams(vmem_limit_bytes=24 * 1024 * 1024)


def dot(left, right, sides, precision=None):
    return lax.dot_general(
        left,
        right,
        (((sides[0],), (sides[1],)), ((), ())),
        precision=precision,
        preferred_element_type=F32,
    )


def iota(shape, axis):
    return lax.broadcasted_iota(jnp.int32, shape, axis)


def call(kernel, outs, scratch=(), flops=1 << 29, moved=1 << 22, scalars=0, arrays=0):
    specs = {}
    if scalars:
        specs["in_specs"] = [pl.BlockSpec(memory_space=pltpu.SMEM)] * scalars + [
            pl.BlockSpec(memory_space=pltpu.VMEM)
        ] * arrays
    return pl.pallas_call(
        kernel,
        **specs,
        out_shape=[jax.ShapeDtypeStruct(shape, dtype) for shape, dtype in outs],
        scratch_shapes=list(scratch),
        compiler_params=LIMIT,
        cost_estimate=pl.CostEstimate(flops=flops, bytes_accessed=moved, transcendentals=0),
    )


def put_blocks(out_refs, at, rows, piece):
    blocks = piece.astype(BF16).reshape(32, rows, LANES)
    each = 32 // len(out_refs)
    for part, out_ref in enumerate(out_refs):
        out_ref[:, pl.ds(at, rows), :] = blocks[part * each : (part + 1) * each]


def put_tiles(out_refs, at, value):
    for tile in range(value.shape[1] // LANES):
        put_blocks(out_refs, (at + tile) * 16, 16, value[:, tile * LANES : (tile + 1) * LANES])


def halves(matrix):
    parts = matrix.reshape(32, 16, matrix.shape[1])
    return [parts[:, low : low + 8].reshape(256, -1).astype(BF16) for low in (0, 8)]


def put_rest(out_refs, matrix, rest):
    low, high = halves(matrix)
    none = jnp.zeros_like(rest)
    packed = dot(low, jnp.concatenate([rest, none], 0), (1, 1)) + dot(
        high, jnp.concatenate([none, rest], 0), (1, 1)
    )
    put_blocks(out_refs, 112, 8, packed)


def get_tiles(in_ref, held_ref):
    for tile in range(7):
        held_ref[:, tile * LANES : (tile + 1) * LANES] = in_ref[:, pl.ds(tile * 16, 16), :].reshape(512, LANES)
    rest = in_ref[:, pl.ds(112, 8), :].astype(F32)
    first = iota(rest.shape, 2) < 64
    low = jnp.where(first, rest, 0.0)
    high = jnp.where(first, pltpu.roll(rest, 64, 2), 0.0)
    whole = jnp.concatenate([low, high], 1).reshape(512, LANES)
    held_ref[:, 7 * LANES :] = whole.astype(BF16)


def owner(place_ref, y, zh, c):
    return (
        lax.rem(place_ref[0] + y, 4) * 8 + lax.rem(place_ref[1] + zh, 4) * 2 + lax.rem(place_ref[2] + c, 2)
    )


def edge_kernel(frames_ref, edge_ref):
    pick = (iota((16, LANES), 1) == iota((16, LANES), 0) + 112).astype(BF16)
    edge_ref[...] = dot(pick, frames_ref[:, 384:], (1, 1)).astype(BF16)


def widened(right_ref):
    row, column = iota((512, 512), 0), iota((512, 512), 1)
    order = (column == (row % 16) * 32 + row // 16).astype(BF16)
    repeat = (iota((32, 512), 0) == iota((32, 512), 1) % 32).astype(BF16)
    tall = dot(order, right_ref[...], (1, 0)).astype(BF16)
    return jnp.where(column // 32 == row % 16, dot(tall, repeat, (1, 0)), 0.0)


def gated(frames_ref, grad_ref, here):
    x = frames_ref[here, :].astype(F32)
    cot = grad_ref[here, :].astype(F32)
    return (cot * (x * jax.nn.sigmoid(x))).astype(BF16)


def back_kernel(frames_ref, grad_ref, right_ref, out_ref):
    wide = widened(right_ref)
    narrow = wide.astype(BF16)
    for at in range(0, 960, 256):
        rows = min(256, 960 - at)
        dsecond = gated(frames_ref, grad_ref, pl.ds(at, rows))
        whole = rows // LANES * LANES
        put_tiles([out_ref], at // LANES, dot(narrow, dsecond[:whole], (1, 1)))
        if rows > whole:
            put_rest([out_ref], wide, dsecond[whole:])


def wide_kernel(right_ref, wide_ref):
    wide_ref[...] = widened(right_ref).astype(BF16)


def front_gate_kernel(frames_ref, grad_ref, dsecond_ref):
    for at in range(0, 512, 128):
        dsecond_ref[pl.ds(at, 128), :] = gated(frames_ref, grad_ref, pl.ds(at, 128))


def rear_gate_kernel(frames_ref, grad_ref, dsecond_ref):
    for at in range(0, 448, 64):
        dsecond_ref[pl.ds(at, 64), :] = gated(frames_ref, grad_ref, pl.ds(512 + at, 64))
    dsecond_ref[448:, :] = jnp.zeros((64, 512), BF16)


def conv_kernel(place_ref, frames_ref, edge_ref, taps_ref, left_ref, conv_ref, near_ref, far_ref, turned_ref, order_ref):
    place = (iota((16, LANES), 1) == iota((16, LANES), 0) + 112).astype(BF16)
    lane = iota((96, LANES), 1)
    for clip in range(CLIPS):
        here = pl.ds(clip * 96, 96)
        x = frames_ref[here, :].astype(F32)
        before = dot(edge_ref[:, clip * 96 : (clip + 1) * 96], place, (0, 0))
        total = taps_ref[:, 0:1] * x
        for step in range(1, TAPS):
            moved = pltpu.roll(x, step, 1)
            start = jnp.where(lane < step, pltpu.roll(before, step, 1), moved[:, :LANES])
            total = total + taps_ref[:, step : step + 1] * jnp.concatenate([start, moved[:, LANES:]], 1)
        conv_ref[here, :] = total.astype(BF16)
    conv_ref[960:, :] = jnp.zeros((64, 512), BF16)
    turned_ref[...] = left_ref[...].astype(F32).T.reshape(32, 16, 512)
    for block in range(32):
        order_ref[block] = turned_ref[owner(place_ref, block // 4 % 4, block % 4, block // 16)]
    turned = order_ref[...].reshape(512, 512)
    narrow = turned.astype(BF16)
    for at in range(0, 960, 256):
        rows = min(256, 960 - at)
        whole = rows // LANES * LANES
        conv = conv_ref[pl.ds(at, rows), :]
        put_tiles([near_ref, far_ref], at // LANES, dot(narrow, conv[:whole], (1, 1)))
        if rows > whole:
            put_rest([near_ref, far_ref], turned, conv[whole:])


def left_kernel(in_ref, conv_ref, left_ref, part_ref, dfirst_ref, edge_ref):
    get_tiles(in_ref, dfirst_ref)
    edge_ref[...] = dot(left_ref[0:16, :], dfirst_ref[...], (1, 0))[0:8]
    part_ref[...] = dot(conv_ref[...], dfirst_ref[...], (0, 1))


def dconv_kernel(dfirst_ref, taps_ref, left_ref, back_ref):
    dconv = dot(dfirst_ref[...], left_ref[...], (0, 1))
    lane = iota((96, LANES), 1)
    for clip in range(CLIPS):
        y = dconv[clip * 96 : (clip + 1) * 96]
        total = taps_ref[:, 0:1] * y
        for step in range(1, TAPS):
            moved = pltpu.roll(y, 512 - step, 1)
            end = jnp.where(lane < LANES - step, moved[:, 384:], 0.0)
            total = total + taps_ref[:, step : step + 1] * jnp.concatenate([moved[:, :384], end], 1)
        back_ref[pl.ds(clip * 96, 96), :] = total


def right_kernel(place_ref, in0_ref, in1_ref, in2_ref, in3_ref, front_ref, rear_ref, part_ref, first_ref):
    for zh, in_ref in enumerate((in0_ref, in1_ref, in2_ref, in3_ref)):
        rest = in_ref[:, pl.ds(112, 8), :].astype(F32)
        begin = iota(rest.shape, 2) < 64
        low = jnp.where(begin, rest, 0.0)
        high = jnp.where(begin, pltpu.roll(rest, 64, 2), 0.0)
        last = jnp.concatenate([low, high], 1).astype(BF16)
        for block in range(8):
            source = owner(place_ref, 4 - block // 2, 4 - zh, 2 - block % 2)
            for tile in range(7):
                first_ref[source, :, tile * LANES : (tile + 1) * LANES] = in_ref[block, pl.ds(tile * 16, 16), :]
            first_ref[source, :, 7 * LANES :] = last[block]
    for at in range(0, 512, 128):
        rows = first_ref[pl.ds(at // 16, 8)].reshape(128, 1024)
        full = dot(rows[:, :512], front_ref[...], (1, 0)) + dot(rows[:, 512:], rear_ref[...], (1, 0))
        kept = jnp.where(iota(full.shape, 1) // 32 == iota(full.shape, 0) % 16, full, 0.0)
        total = jnp.sum(kept.reshape(8, 16, 512), 1)
        for tile in range(4):
            part_ref[pl.ds(at // 4 + tile, 8, stride=4), :] = total[:, tile * LANES : (tile + 1) * LANES]


def end_kernel(first_ref, wide_ref, frames_ref, grad_ref, back_ref, after_ref, taps_ref, mixed_ref, out_ref):
    place = (iota((8, LANES), 1) == iota((8, LANES), 0)).astype(F32)
    lane = iota((96, LANES), 1)
    second = dot(first_ref[...].reshape(512, 1024), wide_ref[...], (0, 0))
    for clip in range(CLIPS):
        here = pl.ds(clip * 96, 96)
        x = frames_ref[here, :].astype(F32)
        cot = grad_ref[here, :].astype(F32)
        sig = jax.nn.sigmoid(x)
        sec = second[clip * 96 : (clip + 1) * 96]
        mixed_ref[here, :] = (sec * (x * sig)).astype(BF16)
        total = cot * sec * sig * (1.0 + x * (1.0 - sig)) + back_ref[here, :]
        after = dot(after_ref[:, clip * 96 : (clip + 1) * 96], place, (0, 0), HIGHEST)
        end = total[:, 384:]
        for step in range(1, TAPS):
            term = taps_ref[:, step : step + 1] * pltpu.roll(after, LANES - step, 1)
            end = end + jnp.where(lane >= LANES - step, term, 0.0)
        out_ref[here, :] = jnp.concatenate([total[:, :384], end], 1).astype(BF16)


def exchange(value, axes):
    return lax.all_to_all(value, axes, split_axis=0, concat_axis=0, tiled=True)


def along_seq(value, steps):
    pairs = [(s, s + steps) for s in range(32) if 0 <= s + steps < 32]
    return lax.ppermute(value, SEQ, pairs)


def ahead(value, axis, step):
    count = lax.axis_size(axis)
    return lax.ppermute(value, axis, [(s, (s + step) % count) for s in range(count)])


def gather_rows(near, far):
    shape = (4, 4, 120, LANES)
    near, far = near.reshape(shape), ahead(far, "c", 1).reshape(shape)
    both = [jnp.stack([near[step], far[step]]) for step in range(4)]
    both = [both[0]] + [ahead(both[step], "y", step) for step in range(1, 4)]
    return [jnp.stack([part[:, step] for part in both]).reshape(8, 120, LANES) for step in range(4)]


def halved(part, axis, apart):
    rows = part.shape[0] // 2
    upper = lax.axis_index(axis) // apart % 2
    mine = lax.dynamic_slice_in_dim(part, upper * rows, rows, 0)
    other = lax.dynamic_slice_in_dim(part, (1 - upper) * rows, rows, 0)
    return mine + lax.ppermute(other, axis, [(s, s ^ apart) for s in range(lax.axis_size(axis))])


def summed(part, axis):
    count = lax.axis_size(axis)
    me = lax.axis_index(axis)
    rows = part.shape[0] // count

    def quarter(step):
        return lax.dynamic_slice_in_dim(part, lax.rem(me + step, count) * rows, rows, 0)

    arrived = [ahead(quarter(step), axis, step) for step in range(1, count)]
    return functools.reduce(jnp.add, arrived, quarter(0))


def total_kernel(in_ref, out_ref):
    total = jnp.sum(in_ref[...], 0)
    for row in range(8):
        for group in range(4):
            piece = total[row : row + 1, group * 32 : group * 32 + 32]
            out_ref[row % 4 * 4 + group, row // 4 : row // 4 + 1, :] = piece


def shards(frames, conv_taps, left_factor, right_factor, out_grad):
    x = frames.reshape(960, 512)
    cot = out_grad.reshape(960, 512)
    left = left_factor.reshape(512, 512)
    taps = conv_taps.T
    blocks = ((32, 120, LANES), BF16)

    (edge,) = call(edge_kernel, [((16, 960), BF16)])(x)
    edge = along_seq(edge, 1)
    right = right_factor.reshape(512, 32)
    (sent_back,) = call(back_kernel, [blocks])(x, cot, right)
    sent_back, edge = lax.optimization_barrier((sent_back, edge))
    back = exchange(sent_back, SEQ)
    place = jnp.stack([lax.axis_index(axis) for axis in SEQ]).astype(jnp.int32)
    part = ((16, 120, LANES), BF16)
    conv, near, far = call(
        conv_kernel,
        [((1024, 512), BF16), part, part],
        scratch=[pltpu.VMEM((32, 16, 512), F32)] * 2,
        scalars=1,
        arrays=4,
    )(place, x, edge, taps, left)
    rows = gather_rows(near, far)
    columns = [rows[0]] + [ahead(rows[step], "zh", step) for step in range(1, 4)]

    left_part, dfirst, dedge = call(left_kernel, [((512, 512), F32), ((512, 1024), BF16), ((8, 1024), F32)])(
        back, conv, left
    )
    after = along_seq(dedge, -1)
    left_sum = jnp.sum(exchange(left_part.reshape(4, 128, 512), "x"), 0)
    left_grad = halved(halved(left_sum, "zl", 2), "zl", 1)
    (conv_back,) = call(dconv_kernel, [((960, 512), F32)], flops=1 << 35)(dfirst, taps, left)
    late = lax.optimization_barrier((x, cot, right, dedge))
    (wide,) = call(wide_kernel, [((512, 512), BF16)], flops=1 << 35)(late[2])
    (front,) = call(front_gate_kernel, [((512, 512), BF16)], flops=1 << 35)(*late[:2])
    (rear,) = call(rear_gate_kernel, [((512, 512), BF16)], flops=1 << 35)(*late[:2])
    columns, left_grad, after, conv_back, front, rear, wide = lax.optimization_barrier(
        (columns, left_grad, after, conv_back, front, rear, wide)
    )

    right_part, first = call(right_kernel, [((128, LANES), F32), ((32, 16, 1024), BF16)], scalars=1, arrays=6)(
        place, *columns, front, rear
    )
    right_all = exchange(right_part.reshape(16, 8, LANES), CHAN)
    mixed, frames_grad = call(end_kernel, [((960, 512), BF16), ((960, 512), BF16)])(
        first, wide, x, cot, conv_back, after, taps
    )
    (right_grad,) = call(total_kernel, [((16, 2, 32), F32)])(right_all)
    return (
        mixed.reshape(frames.shape),
        frames_grad.reshape(frames.shape),
        left_grad.reshape(1, 32, 512),
        right_grad,
    )


def solution(mesh):
    fine = Mesh(mesh.devices.reshape(4, 4, 2, 4, 4), SEQ + CHAN)
    placed = (
        P(None, CHAN, SEQ),
        P(None, CHAN),
        P(SEQ, None, None),
        P(SEQ, None, None),
        P(None, CHAN, SEQ),
    )
    return jax.shard_map(
        shards,
        mesh=fine,
        in_specs=placed,
        out_specs=(
            P(None, CHAN, SEQ),
            P(None, CHAN, SEQ),
            P(SEQ, CHAN, None),
            P(SEQ, CHAN, None),
        ),
        check_vma=False,
    )
```

```python
import jax
import jax.numpy as jnp
from jax import lax
from jax.experimental import pallas as pl
from jax.experimental.pallas import tpu as pltpu
from jax.sharding import Mesh
from jax.sharding import PartitionSpec as P

TAPS = 4
CLIPS = 10
LANES = 128
SEQ = ("y", "zh", "c")
CHAN = ("x", "zl")
F32 = jnp.float32
BF16 = jnp.bfloat16
HIGHEST = lax.Precision.HIGHEST
LIMIT = pltpu.CompilerParams(vmem_limit_bytes=24 * 1024 * 1024)


def dot(left, right, sides, precision=None):
    return lax.dot_general(
        left,
        right,
        (((sides[0],), (sides[1],)), ((), ())),
        precision=precision,
        preferred_element_type=F32,
    )


def iota(shape, axis):
    return lax.broadcasted_iota(jnp.int32, shape, axis)


def call(kernel, outs, scratch=(), flops=1 << 29, moved=1 << 22, scalars=0, arrays=0):
    specs = {}
    if scalars:
        specs["in_specs"] = [pl.BlockSpec(memory_space=pltpu.SMEM)] * scalars + [
            pl.BlockSpec(memory_space=pltpu.VMEM)
        ] * arrays
    return pl.pallas_call(
        kernel,
        **specs,
        out_shape=[jax.ShapeDtypeStruct(shape, dtype) for shape, dtype in outs],
        scratch_shapes=list(scratch),
        compiler_params=LIMIT,
        cost_estimate=pl.CostEstimate(flops=flops, bytes_accessed=moved, transcendentals=0),
    )


def put_blocks(out_refs, at, rows, piece):
    blocks = piece.astype(BF16).reshape(32, rows, LANES)
    each = 32 // len(out_refs)
    for part, out_ref in enumerate(out_refs):
        out_ref[:, pl.ds(at, rows), :] = blocks[part * each : (part + 1) * each]


def put_tiles(out_refs, at, value):
    for tile in range(value.shape[1] // LANES):
        put_blocks(out_refs, (at + tile) * 16, 16, value[:, tile * LANES : (tile + 1) * LANES])


def halves(matrix):
    parts = matrix.reshape(32, 16, matrix.shape[1])
    return [parts[:, low : low + 8].reshape(256, -1).astype(BF16) for low in (0, 8)]


def put_rest(out_refs, matrix, rest):
    low, high = halves(matrix)
    none = jnp.zeros_like(rest)
    packed = dot(low, jnp.concatenate([rest, none], 0), (1, 1)) + dot(
        high, jnp.concatenate([none, rest], 0), (1, 1)
    )
    put_blocks(out_refs, 112, 8, packed)


def get_tiles(in_ref, held_ref):
    for tile in range(7):
        held_ref[:, tile * LANES : (tile + 1) * LANES] = in_ref[:, pl.ds(tile * 16, 16), :].reshape(512, LANES)
    rest = in_ref[:, pl.ds(112, 8), :].astype(F32)
    first = iota(rest.shape, 2) < 64
    low = jnp.where(first, rest, 0.0)
    high = jnp.where(first, pltpu.roll(rest, 64, 2), 0.0)
    whole = jnp.concatenate([low, high], 1).reshape(512, LANES)
    held_ref[:, 7 * LANES :] = whole.astype(BF16)


def owner(place_ref, y, zh, c):
    return (
        lax.rem(place_ref[0] + y, 4) * 8 + lax.rem(place_ref[1] + zh, 4) * 2 + lax.rem(place_ref[2] + c, 2)
    )


def edge_kernel(frames_ref, edge_ref):
    pick = (iota((16, LANES), 1) == iota((16, LANES), 0) + 112).astype(BF16)
    edge_ref[...] = dot(pick, frames_ref[:, 384:], (1, 1)).astype(BF16)


def widened(right_ref):
    row, column = iota((512, 512), 0), iota((512, 512), 1)
    order = (column == (row % 16) * 32 + row // 16).astype(BF16)
    repeat = (iota((32, 512), 0) == iota((32, 512), 1) % 32).astype(BF16)
    tall = dot(order, right_ref[...], (1, 0)).astype(BF16)
    return jnp.where(column // 32 == row % 16, dot(tall, repeat, (1, 0)), 0.0)


def gated(frames_ref, grad_ref, here):
    x = frames_ref[here, :].astype(F32)
    cot = grad_ref[here, :].astype(F32)
    return (cot * (x * jax.nn.sigmoid(x))).astype(BF16)


def back_kernel(frames_ref, grad_ref, right_ref, out_ref):
    wide = widened(right_ref)
    narrow = wide.astype(BF16)
    for at in range(0, 960, 256):
        rows = min(256, 960 - at)
        dsecond = gated(frames_ref, grad_ref, pl.ds(at, rows))
        whole = rows // LANES * LANES
        put_tiles([out_ref], at // LANES, dot(narrow, dsecond[:whole], (1, 1)))
        if rows > whole:
            put_rest([out_ref], wide, dsecond[whole:])


def wide_kernel(right_ref, wide_ref):
    wide_ref[...] = widened(right_ref).astype(BF16)


def front_gate_kernel(frames_ref, grad_ref, dsecond_ref):
    for at in range(0, 512, 128):
        dsecond_ref[pl.ds(at, 128), :] = gated(frames_ref, grad_ref, pl.ds(at, 128))


def rear_gate_kernel(frames_ref, grad_ref, dsecond_ref):
    for at in range(0, 448, 64):
        dsecond_ref[pl.ds(at, 64), :] = gated(frames_ref, grad_ref, pl.ds(512 + at, 64))
    dsecond_ref[448:, :] = jnp.zeros((64, 512), BF16)


def conv_kernel(place_ref, frames_ref, edge_ref, taps_ref, left_ref, conv_ref, near_ref, far_ref, turned_ref, order_ref):
    place = (iota((16, LANES), 1) == iota((16, LANES), 0) + 112).astype(BF16)
    lane = iota((96, LANES), 1)
    for clip in range(CLIPS):
        here = pl.ds(clip * 96, 96)
        x = frames_ref[here, :].astype(F32)
        before = dot(edge_ref[:, clip * 96 : (clip + 1) * 96], place, (0, 0))
        total = taps_ref[:, 0:1] * x
        for step in range(1, TAPS):
            moved = pltpu.roll(x, step, 1)
            start = jnp.where(lane < step, pltpu.roll(before, step, 1), moved[:, :LANES])
            total = total + taps_ref[:, step : step + 1] * jnp.concatenate([start, moved[:, LANES:]], 1)
        conv_ref[here, :] = total.astype(BF16)
    conv_ref[960:, :] = jnp.zeros((64, 512), BF16)
    turned_ref[...] = left_ref[...].astype(F32).T.reshape(32, 16, 512)
    for block in range(32):
        order_ref[block] = turned_ref[owner(place_ref, block // 4 % 4, block % 4, block // 16)]
    turned = order_ref[...].reshape(512, 512)
    narrow = turned.astype(BF16)
    for at in range(0, 960, 256):
        rows = min(256, 960 - at)
        whole = rows // LANES * LANES
        conv = conv_ref[pl.ds(at, rows), :]
        put_tiles([near_ref, far_ref], at // LANES, dot(narrow, conv[:whole], (1, 1)))
        if rows > whole:
            put_rest([near_ref, far_ref], turned, conv[whole:])


def left_kernel(in_ref, conv_ref, left_ref, part_ref, dfirst_ref, edge_ref):
    get_tiles(in_ref, dfirst_ref)
    edge_ref[...] = dot(left_ref[0:16, :], dfirst_ref[...], (1, 0))[0:8]
    part_ref[...] = dot(conv_ref[...], dfirst_ref[...], (0, 1))


def dconv_kernel(dfirst_ref, taps_ref, left_ref, back_ref):
    dconv = dot(dfirst_ref[...], left_ref[...], (0, 1))
    lane = iota((96, LANES), 1)
    for clip in range(CLIPS):
        y = dconv[clip * 96 : (clip + 1) * 96]
        total = taps_ref[:, 0:1] * y
        for step in range(1, TAPS):
            moved = pltpu.roll(y, 512 - step, 1)
            end = jnp.where(lane < LANES - step, moved[:, 384:], 0.0)
            total = total + taps_ref[:, step : step + 1] * jnp.concatenate([moved[:, :384], end], 1)
        back_ref[pl.ds(clip * 96, 96), :] = total


def right_kernel(place_ref, in0_ref, in1_ref, in2_ref, in3_ref, front_ref, rear_ref, part_ref, first_ref):
    for zh, in_ref in enumerate((in0_ref, in1_ref, in2_ref, in3_ref)):
        rest = in_ref[:, pl.ds(112, 8), :].astype(F32)
        begin = iota(rest.shape, 2) < 64
        low = jnp.where(begin, rest, 0.0)
        high = jnp.where(begin, pltpu.roll(rest, 64, 2), 0.0)
        last = jnp.concatenate([low, high], 1).astype(BF16)
        for block in range(8):
            source = owner(place_ref, 4 - block // 2, 4 - zh, 2 - block % 2)
            for tile in range(7):
                first_ref[source, :, tile * LANES : (tile + 1) * LANES] = in_ref[block, pl.ds(tile * 16, 16), :]
            first_ref[source, :, 7 * LANES :] = last[block]
    for at in range(0, 512, 128):
        rows = first_ref[pl.ds(at // 16, 8)].reshape(128, 1024)
        full = dot(rows[:, :512], front_ref[...], (1, 0)) + dot(rows[:, 512:], rear_ref[...], (1, 0))
        kept = jnp.where(iota(full.shape, 1) // 32 == iota(full.shape, 0) % 16, full, 0.0)
        total = jnp.sum(kept.reshape(8, 16, 512), 1)
        for tile in range(4):
            part_ref[pl.ds(at // 4 + tile, 8, stride=4), :] = total[:, tile * LANES : (tile + 1) * LANES]


def end_kernel(first_ref, wide_ref, frames_ref, grad_ref, back_ref, after_ref, taps_ref, mixed_ref, out_ref):
    place = (iota((8, LANES), 1) == iota((8, LANES), 0)).astype(F32)
    lane = iota((96, LANES), 1)
    second = dot(first_ref[...].reshape(512, 1024), wide_ref[...], (0, 0))
    for clip in range(CLIPS):
        here = pl.ds(clip * 96, 96)
        x = frames_ref[here, :].astype(F32)
        cot = grad_ref[here, :].astype(F32)
        sig = jax.nn.sigmoid(x)
        sec = second[clip * 96 : (clip + 1) * 96]
        mixed_ref[here, :] = (sec * (x * sig)).astype(BF16)
        total = cot * sec * sig * (1.0 + x * (1.0 - sig)) + back_ref[here, :]
        after = dot(after_ref[:, clip * 96 : (clip + 1) * 96], place, (0, 0), HIGHEST)
        end = total[:, 384:]
        for step in range(1, TAPS):
            term = taps_ref[:, step : step + 1] * pltpu.roll(after, LANES - step, 1)
            end = end + jnp.where(lane >= LANES - step, term, 0.0)
        out_ref[here, :] = jnp.concatenate([total[:, :384], end], 1).astype(BF16)


def exchange(value, axes):
    return lax.all_to_all(value, axes, split_axis=0, concat_axis=0, tiled=True)


def along_seq(value, steps):
    pairs = [(s, s + steps) for s in range(32) if 0 <= s + steps < 32]
    return lax.ppermute(value, SEQ, pairs)


def ahead(value, axis, step):
    count = lax.axis_size(axis)
    return lax.ppermute(value, axis, [(s, (s + step) % count) for s in range(count)])


def gather_rows(near, far):
    shape = (4, 4, 120, LANES)
    near, far = near.reshape(shape), ahead(far, "c", 1).reshape(shape)
    both = [jnp.stack([near[step], far[step]]) for step in range(4)]
    both = [both[0]] + [ahead(both[step], "y", step) for step in range(1, 4)]
    return [jnp.stack([part[:, step] for part in both]).reshape(8, 120, LANES) for step in range(4)]


def halves_met(part, axis, apart):
    rows = part.shape[0] // 2
    upper = lax.axis_index(axis) // apart % 2
    mine = lax.dynamic_slice_in_dim(part, upper * rows, rows, 0)
    other = lax.dynamic_slice_in_dim(part, (1 - upper) * rows, rows, 0)
    return mine, lax.ppermute(other, axis, [(s, s ^ apart) for s in range(lax.axis_size(axis))])


def total_kernel(in_ref, out_ref):
    total = jnp.sum(in_ref[...], 0)
    for row in range(8):
        for group in range(4):
            piece = total[row : row + 1, group * 32 : group * 32 + 32]
            out_ref[row % 4 * 4 + group, row // 4 : row // 4 + 1, :] = piece


def shards(frames, conv_taps, left_factor, right_factor, out_grad):
    x = frames.reshape(960, 512)
    cot = out_grad.reshape(960, 512)
    left = left_factor.reshape(512, 512)
    taps = conv_taps.T
    blocks = ((32, 120, LANES), BF16)

    (edge,) = call(edge_kernel, [((16, 960), BF16)])(x)
    edge = along_seq(edge, 1)
    right = right_factor.reshape(512, 32)
    (sent_back,) = call(back_kernel, [blocks])(x, cot, right)
    sent_back, edge = lax.optimization_barrier((sent_back, edge))
    back = exchange(sent_back, SEQ)
    place = jnp.stack([lax.axis_index(axis) for axis in SEQ]).astype(jnp.int32)
    part = ((16, 120, LANES), BF16)
    conv, near, far = call(
        conv_kernel,
        [((1024, 512), BF16), part, part],
        scratch=[pltpu.VMEM((32, 16, 512), F32)] * 2,
        scalars=1,
        arrays=4,
    )(place, x, edge, taps, left)
    rows = gather_rows(near, far)
    columns = [rows[0]] + [ahead(rows[step], "zh", step) for step in range(1, 4)]

    left_part, dfirst, dedge = call(left_kernel, [((512, 512), F32), ((512, 1024), BF16), ((8, 1024), F32)])(
        back, conv, left
    )
    after = along_seq(dedge, -1)
    (conv_back,) = call(dconv_kernel, [((960, 512), F32)], flops=1 << 35)(dfirst, taps, left)
    left_sum = jnp.sum(exchange(left_part.reshape(4, 128, 512), "x"), 0)
    left_sum = lax.optimization_barrier((left_sum, conv_back))[0]
    kept, met = halves_met(left_sum, "zl", 2)
    late = lax.optimization_barrier((x, cot, right, dedge))
    (wide,) = call(wide_kernel, [((512, 512), BF16)], flops=1 << 31)(late[2])
    (front,) = call(front_gate_kernel, [((512, 512), BF16)], flops=1 << 31)(*late[:2])
    (rear,) = call(rear_gate_kernel, [((512, 512), BF16)], flops=1 << 31)(*late[:2])
    columns, after, conv_back, front, rear, wide = lax.optimization_barrier(
        (columns, after, conv_back, front, rear, wide)
    )

    right_part, first = call(right_kernel, [((128, LANES), F32), ((32, 16, 1024), BF16)], scalars=1, arrays=6)(
        place, *columns, front, rear
    )
    right_all = exchange(right_part.reshape(16, 8, LANES), CHAN)
    met = lax.optimization_barrier((met, right_part))[0]
    left_grad = sum(halves_met(kept + met, "zl", 1))
    mixed, frames_grad = call(end_kernel, [((960, 512), BF16), ((960, 512), BF16)])(
        first, wide, x, cot, conv_back, after, taps
    )
    (right_grad,) = call(total_kernel, [((16, 2, 32), F32)])(right_all)
    return (
        mixed.reshape(frames.shape),
        frames_grad.reshape(frames.shape),
        left_grad.reshape(1, 32, 512),
        right_grad,
    )


def solution(mesh):
    fine = Mesh(mesh.devices.reshape(4, 4, 2, 4, 4), SEQ + CHAN)
    placed = (
        P(None, CHAN, SEQ),
        P(None, CHAN),
        P(SEQ, None, None),
        P(SEQ, None, None),
        P(None, CHAN, SEQ),
    )
    return jax.shard_map(
        shards,
        mesh=fine,
        in_specs=placed,
        out_specs=(
            P(None, CHAN, SEQ),
            P(None, CHAN, SEQ),
            P(SEQ, CHAN, None),
            P(SEQ, CHAN, None),
        ),
        check_vma=False,
    )
```

```python
import jax
import jax.numpy as jnp
from jax import lax
from jax.experimental import pallas as pl
from jax.experimental.pallas import tpu as pltpu
from jax.sharding import Mesh
from jax.sharding import PartitionSpec as P

TAPS = 4
CLIPS = 10
LANES = 128
SEQ = ("y", "zh", "c")
CHAN = ("x", "zl")
F32 = jnp.float32
BF16 = jnp.bfloat16
HIGHEST = lax.Precision.HIGHEST
LIMIT = pltpu.CompilerParams(vmem_limit_bytes=24 * 1024 * 1024)


def dot(left, right, sides, precision=None):
    return lax.dot_general(
        left,
        right,
        (((sides[0],), (sides[1],)), ((), ())),
        precision=precision,
        preferred_element_type=F32,
    )


def iota(shape, axis):
    return lax.broadcasted_iota(jnp.int32, shape, axis)


def call(kernel, outs, scratch=(), flops=1 << 29, moved=1 << 22, scalars=0, arrays=0):
    specs = {}
    if scalars:
        specs["in_specs"] = [pl.BlockSpec(memory_space=pltpu.SMEM)] * scalars + [
            pl.BlockSpec(memory_space=pltpu.VMEM)
        ] * arrays
    return pl.pallas_call(
        kernel,
        **specs,
        out_shape=[jax.ShapeDtypeStruct(shape, dtype) for shape, dtype in outs],
        scratch_shapes=list(scratch),
        compiler_params=LIMIT,
        cost_estimate=pl.CostEstimate(flops=flops, bytes_accessed=moved, transcendentals=0),
    )


def put_blocks(out_refs, at, rows, piece):
    blocks = piece.astype(BF16).reshape(32, rows, LANES)
    each = 32 // len(out_refs)
    for part, out_ref in enumerate(out_refs):
        out_ref[:, pl.ds(at, rows), :] = blocks[part * each : (part + 1) * each]


def put_tiles(out_refs, at, value):
    for tile in range(value.shape[1] // LANES):
        put_blocks(out_refs, (at + tile) * 16, 16, value[:, tile * LANES : (tile + 1) * LANES])


def halves(matrix):
    parts = matrix.reshape(32, 16, matrix.shape[1])
    return [parts[:, low : low + 8].reshape(256, -1).astype(BF16) for low in (0, 8)]


def put_rest(out_refs, matrix, rest):
    low, high = halves(matrix)
    none = jnp.zeros_like(rest)
    packed = dot(low, jnp.concatenate([rest, none], 0), (1, 1)) + dot(
        high, jnp.concatenate([none, rest], 0), (1, 1)
    )
    put_blocks(out_refs, 112, 8, packed)


def get_tiles(in_ref, held_ref):
    for tile in range(7):
        held_ref[:, tile * LANES : (tile + 1) * LANES] = in_ref[:, pl.ds(tile * 16, 16), :].reshape(512, LANES)
    rest = in_ref[:, pl.ds(112, 8), :].astype(F32)
    first = iota(rest.shape, 2) < 64
    low = jnp.where(first, rest, 0.0)
    high = jnp.where(first, pltpu.roll(rest, 64, 2), 0.0)
    whole = jnp.concatenate([low, high], 1).reshape(512, LANES)
    held_ref[:, 7 * LANES :] = whole.astype(BF16)


def owner(place_ref, y, zh, c):
    return (
        lax.rem(place_ref[0] + y, 4) * 8 + lax.rem(place_ref[1] + zh, 4) * 2 + lax.rem(place_ref[2] + c, 2)
    )


def edge_kernel(frames_ref, edge_ref):
    pick = (iota((16, LANES), 1) == iota((16, LANES), 0) + 112).astype(BF16)
    edge_ref[...] = dot(pick, frames_ref[:, 384:], (1, 1)).astype(BF16)


def widened(right_ref):
    row, column = iota((512, 512), 0), iota((512, 512), 1)
    order = (column == (row % 16) * 32 + row // 16).astype(BF16)
    repeat = (iota((32, 512), 0) == iota((32, 512), 1) % 32).astype(BF16)
    tall = dot(order, right_ref[...], (1, 0)).astype(BF16)
    return jnp.where(column // 32 == row % 16, dot(tall, repeat, (1, 0)), 0.0)


def gated(frames_ref, grad_ref, here):
    x = frames_ref[here, :].astype(F32)
    cot = grad_ref[here, :].astype(F32)
    return (cot * (x * jax.nn.sigmoid(x))).astype(BF16)


def back_kernel(frames_ref, grad_ref, right_ref, out_ref):
    wide = widened(right_ref)
    narrow = wide.astype(BF16)
    for at in range(0, 960, 256):
        rows = min(256, 960 - at)
        dsecond = gated(frames_ref, grad_ref, pl.ds(at, rows))
        whole = rows // LANES * LANES
        put_tiles([out_ref], at // LANES, dot(narrow, dsecond[:whole], (1, 1)))
        if rows > whole:
            put_rest([out_ref], wide, dsecond[whole:])


def wide_kernel(right_ref, wide_ref):
    wide_ref[...] = widened(right_ref).astype(BF16)


def front_gate_kernel(frames_ref, grad_ref, dsecond_ref):
    for at in range(0, 512, 128):
        dsecond_ref[pl.ds(at, 128), :] = gated(frames_ref, grad_ref, pl.ds(at, 128))


def rear_gate_kernel(frames_ref, grad_ref, dsecond_ref):
    for at in range(0, 448, 64):
        dsecond_ref[pl.ds(at, 64), :] = gated(frames_ref, grad_ref, pl.ds(512 + at, 64))
    dsecond_ref[448:, :] = jnp.zeros((64, 512), BF16)


def conv_kernel(place_ref, frames_ref, edge_ref, taps_ref, left_ref, conv_ref, near_ref, far_ref, turned_ref, order_ref):
    place = (iota((16, LANES), 1) == iota((16, LANES), 0) + 112).astype(BF16)
    lane = iota((96, LANES), 1)
    for clip in range(CLIPS):
        here = pl.ds(clip * 96, 96)
        x = frames_ref[here, :].astype(F32)
        before = dot(edge_ref[:, clip * 96 : (clip + 1) * 96], place, (0, 0))
        total = taps_ref[:, 0:1] * x
        for step in range(1, TAPS):
            moved = pltpu.roll(x, step, 1)
            start = jnp.where(lane < step, pltpu.roll(before, step, 1), moved[:, :LANES])
            total = total + taps_ref[:, step : step + 1] * jnp.concatenate([start, moved[:, LANES:]], 1)
        conv_ref[here, :] = total.astype(BF16)
    conv_ref[960:, :] = jnp.zeros((64, 512), BF16)
    turned_ref[...] = left_ref[...].astype(F32).T.reshape(32, 16, 512)
    for block in range(32):
        order_ref[block] = turned_ref[owner(place_ref, block // 4 % 4, block % 4, block // 16)]
    turned = order_ref[...].reshape(512, 512)
    narrow = turned.astype(BF16)
    for at in range(0, 960, 256):
        rows = min(256, 960 - at)
        whole = rows // LANES * LANES
        conv = conv_ref[pl.ds(at, rows), :]
        put_tiles([near_ref, far_ref], at // LANES, dot(narrow, conv[:whole], (1, 1)))
        if rows > whole:
            put_rest([near_ref, far_ref], turned, conv[whole:])


def left_kernel(in_ref, conv_ref, left_ref, part_ref, dfirst_ref, edge_ref):
    get_tiles(in_ref, dfirst_ref)
    edge_ref[...] = dot(left_ref[0:16, :], dfirst_ref[...], (1, 0))[0:8]
    part_ref[...] = dot(conv_ref[...], dfirst_ref[...], (0, 1))


def dconv_kernel(dfirst_ref, taps_ref, left_ref, back_ref):
    dconv = dot(dfirst_ref[...], left_ref[...], (0, 1))
    lane = iota((96, LANES), 1)
    for clip in range(CLIPS):
        y = dconv[clip * 96 : (clip + 1) * 96]
        total = taps_ref[:, 0:1] * y
        for step in range(1, TAPS):
            moved = pltpu.roll(y, 512 - step, 1)
            end = jnp.where(lane < LANES - step, moved[:, 384:], 0.0)
            total = total + taps_ref[:, step : step + 1] * jnp.concatenate([moved[:, :384], end], 1)
        back_ref[pl.ds(clip * 96, 96), :] = total


def get_columns(place_ref, in_refs, first_ref):
    for zh, in_ref in enumerate(in_refs):
        rest = in_ref[:, pl.ds(112, 8), :].astype(F32)
        begin = iota(rest.shape, 2) < 64
        low = jnp.where(begin, rest, 0.0)
        high = jnp.where(begin, pltpu.roll(rest, 64, 2), 0.0)
        last = jnp.concatenate([low, high], 1).astype(BF16)
        for block in range(8):
            source = owner(place_ref, 4 - block // 2, 4 - zh, 2 - block % 2)
            for tile in range(7):
                first_ref[source, :, tile * LANES : (tile + 1) * LANES] = in_ref[block, pl.ds(tile * 16, 16), :]
            first_ref[source, :, 7 * LANES :] = last[block]


def right_kernel(place_ref, in0_ref, in1_ref, in2_ref, in3_ref, front_ref, rear_ref, part_ref, first_ref):
    get_columns(place_ref, (in0_ref, in1_ref, in2_ref, in3_ref), first_ref)
    for at in range(0, 512, 128):
        rows = first_ref[pl.ds(at // 16, 8)].reshape(128, 1024)
        full = dot(rows[:, :512], front_ref[...], (1, 0)) + dot(rows[:, 512:], rear_ref[...], (1, 0))
        kept = jnp.where(iota(full.shape, 1) // 32 == iota(full.shape, 0) % 16, full, 0.0)
        total = jnp.sum(kept.reshape(8, 16, 512), 1)
        for tile in range(4):
            part_ref[pl.ds(at // 4 + tile, 8, stride=4), :] = total[:, tile * LANES : (tile + 1) * LANES]


def end_kernel(place_ref, in0_ref, in1_ref, in2_ref, in3_ref, wide_ref, frames_ref, grad_ref, back_ref, after_ref, taps_ref, mixed_ref, out_ref, first_ref):
    get_columns(place_ref, (in0_ref, in1_ref, in2_ref, in3_ref), first_ref)
    place = (iota((8, LANES), 1) == iota((8, LANES), 0)).astype(F32)
    lane = iota((96, LANES), 1)
    second = dot(first_ref[...].reshape(512, 1024), wide_ref[...], (0, 0))
    for clip in range(CLIPS):
        here = pl.ds(clip * 96, 96)
        x = frames_ref[here, :].astype(F32)
        cot = grad_ref[here, :].astype(F32)
        sig = jax.nn.sigmoid(x)
        sec = second[clip * 96 : (clip + 1) * 96]
        mixed_ref[here, :] = (sec * (x * sig)).astype(BF16)
        total = cot * sec * sig * (1.0 + x * (1.0 - sig)) + back_ref[here, :]
        after = dot(after_ref[:, clip * 96 : (clip + 1) * 96], place, (0, 0), HIGHEST)
        end = total[:, 384:]
        for step in range(1, TAPS):
            term = taps_ref[:, step : step + 1] * pltpu.roll(after, LANES - step, 1)
            end = end + jnp.where(lane >= LANES - step, term, 0.0)
        out_ref[here, :] = jnp.concatenate([total[:, :384], end], 1).astype(BF16)


def exchange(value, axes):
    return lax.all_to_all(value, axes, split_axis=0, concat_axis=0, tiled=True)


def along_seq(value, steps):
    pairs = [(s, s + steps) for s in range(32) if 0 <= s + steps < 32]
    return lax.ppermute(value, SEQ, pairs)


def ahead(value, axis, step):
    count = lax.axis_size(axis)
    return lax.ppermute(value, axis, [(s, (s + step) % count) for s in range(count)])


def gather_rows(near, far):
    shape = (4, 4, 120, LANES)
    near, far = near.reshape(shape), ahead(far, "c", 1).reshape(shape)
    both = [jnp.stack([near[step], far[step]]) for step in range(4)]
    both = [both[0]] + [ahead(both[step], "y", step) for step in range(1, 4)]
    return [jnp.stack([part[:, step] for part in both]).reshape(8, 120, LANES) for step in range(4)]


def halves_met(part, axis, apart):
    rows = part.shape[0] // 2
    upper = lax.axis_index(axis) // apart % 2
    mine = lax.dynamic_slice_in_dim(part, upper * rows, rows, 0)
    other = lax.dynamic_slice_in_dim(part, (1 - upper) * rows, rows, 0)
    return mine, lax.ppermute(other, axis, [(s, s ^ apart) for s in range(lax.axis_size(axis))])


def total_kernel(in_ref, out_ref):
    total = jnp.sum(in_ref[...], 0)
    for row in range(8):
        for group in range(4):
            piece = total[row : row + 1, group * 32 : group * 32 + 32]
            out_ref[row % 4 * 4 + group, row // 4 : row // 4 + 1, :] = piece


def shards(frames, conv_taps, left_factor, right_factor, out_grad):
    x = frames.reshape(960, 512)
    cot = out_grad.reshape(960, 512)
    left = left_factor.reshape(512, 512)
    taps = conv_taps.T
    blocks = ((32, 120, LANES), BF16)

    (edge,) = call(edge_kernel, [((16, 960), BF16)])(x)
    edge = along_seq(edge, 1)
    right = right_factor.reshape(512, 32)
    (sent_back,) = call(back_kernel, [blocks])(x, cot, right)
    sent_back, edge = lax.optimization_barrier((sent_back, edge))
    back = exchange(sent_back, SEQ)
    place = jnp.stack([lax.axis_index(axis) for axis in SEQ]).astype(jnp.int32)
    part = ((16, 120, LANES), BF16)
    conv, near, far = call(
        conv_kernel,
        [((1024, 512), BF16), part, part],
        scratch=[pltpu.VMEM((32, 16, 512), F32)] * 2,
        scalars=1,
        arrays=4,
    )(place, x, edge, taps, left)
    rows = gather_rows(near, far)
    columns = [rows[0]] + [ahead(rows[step], "zh", step) for step in range(1, 4)]

    left_part, dfirst, dedge = call(left_kernel, [((512, 512), F32), ((512, 1024), BF16), ((8, 1024), F32)])(
        back, conv, left
    )
    after = along_seq(dedge, -1)
    (conv_back,) = call(dconv_kernel, [((960, 512), F32)], flops=1 << 35)(dfirst, taps, left)
    left_sum = jnp.sum(exchange(left_part.reshape(4, 128, 512), "x"), 0)
    left_sum = lax.optimization_barrier((left_sum, conv_back))[0]
    kept, met = halves_met(left_sum, "zl", 2)
    late = lax.optimization_barrier((x, cot, right, dedge))
    (wide,) = call(wide_kernel, [((512, 512), BF16)], flops=1 << 31)(late[2])
    (front,) = call(front_gate_kernel, [((512, 512), BF16)], flops=1 << 31)(*late[:2])
    (rear,) = call(rear_gate_kernel, [((512, 512), BF16)], flops=1 << 31)(*late[:2])
    columns, after, conv_back, front, rear, wide = lax.optimization_barrier(
        (columns, after, conv_back, front, rear, wide)
    )

    scratch = [pltpu.VMEM((32, 16, 1024), BF16)]
    (right_part,) = call(right_kernel, [((128, LANES), F32)], scratch=scratch, scalars=1, arrays=6)(
        place, *columns, front, rear
    )
    right_all = exchange(right_part.reshape(16, 8, LANES), CHAN)
    met = lax.optimization_barrier((met, right_part))[0]
    left_grad = sum(halves_met(kept + met, "zl", 1))
    mixed, frames_grad = call(
        end_kernel, [((960, 512), BF16), ((960, 512), BF16)], scratch=scratch, scalars=1, arrays=10
    )(place, *columns, wide, x, cot, conv_back, after, taps)
    (right_grad,) = call(total_kernel, [((16, 2, 32), F32)])(right_all)
    return (
        mixed.reshape(frames.shape),
        frames_grad.reshape(frames.shape),
        left_grad.reshape(1, 32, 512),
        right_grad,
    )


def solution(mesh):
    fine = Mesh(mesh.devices.reshape(4, 4, 2, 4, 4), SEQ + CHAN)
    placed = (
        P(None, CHAN, SEQ),
        P(None, CHAN),
        P(SEQ, None, None),
        P(SEQ, None, None),
        P(None, CHAN, SEQ),
    )
    return jax.shard_map(
        shards,
        mesh=fine,
        in_specs=placed,
        out_specs=(
            P(None, CHAN, SEQ),
            P(None, CHAN, SEQ),
            P(SEQ, CHAN, None),
            P(SEQ, CHAN, None),
        ),
        check_vma=False,
    )
```

```python
import jax
import jax.numpy as jnp
from jax import lax
from jax.experimental import pallas as pl
from jax.experimental.pallas import tpu as pltpu
from jax.sharding import Mesh
from jax.sharding import PartitionSpec as P

TAPS = 4
CLIPS = 10
LANES = 128
SEQ = ("y", "zh", "c")
CHAN = ("x", "zl")
F32 = jnp.float32
BF16 = jnp.bfloat16
HIGHEST = lax.Precision.HIGHEST
LIMIT = pltpu.CompilerParams(vmem_limit_bytes=24 * 1024 * 1024)


def dot(left, right, sides, precision=None):
    return lax.dot_general(
        left,
        right,
        (((sides[0],), (sides[1],)), ((), ())),
        precision=precision,
        preferred_element_type=F32,
    )


def iota(shape, axis):
    return lax.broadcasted_iota(jnp.int32, shape, axis)


def call(kernel, outs, scratch=(), flops=1 << 29, moved=1 << 22, scalars=0, arrays=0):
    specs = {}
    if scalars:
        specs["in_specs"] = [pl.BlockSpec(memory_space=pltpu.SMEM)] * scalars + [
            pl.BlockSpec(memory_space=pltpu.VMEM)
        ] * arrays
    return pl.pallas_call(
        kernel,
        **specs,
        out_shape=[jax.ShapeDtypeStruct(shape, dtype) for shape, dtype in outs],
        scratch_shapes=list(scratch),
        compiler_params=LIMIT,
        cost_estimate=pl.CostEstimate(flops=flops, bytes_accessed=moved, transcendentals=0),
    )


def put_blocks(out_refs, at, rows, piece):
    blocks = piece.astype(BF16).reshape(32, rows, LANES)
    each = 32 // len(out_refs)
    for part, out_ref in enumerate(out_refs):
        out_ref[:, pl.ds(at, rows), :] = blocks[part * each : (part + 1) * each]


def put_tiles(out_refs, at, value):
    for tile in range(value.shape[1] // LANES):
        put_blocks(out_refs, (at + tile) * 16, 16, value[:, tile * LANES : (tile + 1) * LANES])


def halves(matrix):
    parts = matrix.reshape(32, 16, matrix.shape[1])
    return [parts[:, low : low + 8].reshape(256, -1).astype(BF16) for low in (0, 8)]


def put_rest(out_refs, matrix, rest):
    low, high = halves(matrix)
    none = jnp.zeros_like(rest)
    packed = dot(low, jnp.concatenate([rest, none], 0), (1, 1)) + dot(
        high, jnp.concatenate([none, rest], 0), (1, 1)
    )
    put_blocks(out_refs, 112, 8, packed)


def get_tiles(in_ref, held_ref):
    for tile in range(7):
        held_ref[:, tile * LANES : (tile + 1) * LANES] = in_ref[:, pl.ds(tile * 16, 16), :].reshape(512, LANES)
    rest = in_ref[:, pl.ds(112, 8), :].astype(F32)
    first = iota(rest.shape, 2) < 64
    low = jnp.where(first, rest, 0.0)
    high = jnp.where(first, pltpu.roll(rest, 64, 2), 0.0)
    whole = jnp.concatenate([low, high], 1).reshape(512, LANES)
    held_ref[:, 7 * LANES :] = whole.astype(BF16)


def owner(place_ref, y, zh, c):
    return (
        lax.rem(place_ref[0] + y, 4) * 8 + lax.rem(place_ref[1] + zh, 4) * 2 + lax.rem(place_ref[2] + c, 2)
    )


def edge_kernel(frames_ref, edge_ref):
    pick = (iota((16, LANES), 1) == iota((16, LANES), 0) + 112).astype(BF16)
    edge_ref[...] = dot(pick, frames_ref[:, 384:], (1, 1)).astype(BF16)


def widened(right_ref):
    row, column = iota((512, 512), 0), iota((512, 512), 1)
    order = (column == (row % 16) * 32 + row // 16).astype(BF16)
    repeat = (iota((32, 512), 0) == iota((32, 512), 1) % 32).astype(BF16)
    tall = dot(order, right_ref[...], (1, 0)).astype(BF16)
    return jnp.where(column // 32 == row % 16, dot(tall, repeat, (1, 0)), 0.0)


def gated(frames_ref, grad_ref, here):
    x = frames_ref[here, :].astype(F32)
    cot = grad_ref[here, :].astype(F32)
    return (cot * (x * jax.nn.sigmoid(x))).astype(BF16)


def back_kernel(frames_ref, grad_ref, right_ref, out_ref):
    wide = widened(right_ref)
    narrow = wide.astype(BF16)
    for at in range(0, 960, 256):
        rows = min(256, 960 - at)
        dsecond = gated(frames_ref, grad_ref, pl.ds(at, rows))
        whole = rows // LANES * LANES
        put_tiles([out_ref], at // LANES, dot(narrow, dsecond[:whole], (1, 1)))
        if rows > whole:
            put_rest([out_ref], wide, dsecond[whole:])


def wide_kernel(right_ref, wide_ref):
    wide_ref[...] = widened(right_ref).astype(BF16)


def front_gate_kernel(frames_ref, grad_ref, dsecond_ref):
    for at in range(0, 512, 128):
        dsecond_ref[pl.ds(at, 128), :] = gated(frames_ref, grad_ref, pl.ds(at, 128))


def rear_gate_kernel(frames_ref, grad_ref, dsecond_ref):
    for at in range(0, 448, 64):
        dsecond_ref[pl.ds(at, 64), :] = gated(frames_ref, grad_ref, pl.ds(512 + at, 64))
    dsecond_ref[448:, :] = jnp.zeros((64, 512), BF16)


def conv_kernel(place_ref, frames_ref, edge_ref, taps_ref, left_ref, conv_ref, near_ref, far_ref, turned_ref, order_ref):
    place = (iota((16, LANES), 1) == iota((16, LANES), 0) + 112).astype(BF16)
    lane = iota((96, LANES), 1)
    for clip in range(CLIPS):
        here = pl.ds(clip * 96, 96)
        x = frames_ref[here, :].astype(F32)
        before = dot(edge_ref[:, clip * 96 : (clip + 1) * 96], place, (0, 0))
        total = taps_ref[:, 0:1] * x
        for step in range(1, TAPS):
            moved = pltpu.roll(x, step, 1)
            start = jnp.where(lane < step, pltpu.roll(before, step, 1), moved[:, :LANES])
            total = total + taps_ref[:, step : step + 1] * jnp.concatenate([start, moved[:, LANES:]], 1)
        conv_ref[here, :] = total.astype(BF16)
    conv_ref[960:, :] = jnp.zeros((64, 512), BF16)
    turned_ref[...] = left_ref[...].astype(F32).T.reshape(32, 16, 512)
    for block in range(32):
        order_ref[block] = turned_ref[owner(place_ref, block // 4 % 4, block % 4, block // 16)]
    turned = order_ref[...].reshape(512, 512)
    narrow = turned.astype(BF16)
    for at in range(0, 960, 256):
        rows = min(256, 960 - at)
        whole = rows // LANES * LANES
        conv = conv_ref[pl.ds(at, rows), :]
        put_tiles([near_ref, far_ref], at // LANES, dot(narrow, conv[:whole], (1, 1)))
        if rows > whole:
            put_rest([near_ref, far_ref], turned, conv[whole:])


def left_kernel(in_ref, conv_ref, left_ref, part_ref, dfirst_ref, edge_ref):
    get_tiles(in_ref, dfirst_ref)
    edge_ref[...] = dot(left_ref[0:16, :], dfirst_ref[...], (1, 0))[0:8]
    part_ref[...] = dot(conv_ref[...], dfirst_ref[...], (0, 1))


def dconv_kernel(dfirst_ref, taps_ref, left_ref, back_ref):
    dconv = dot(dfirst_ref[...], left_ref[...], (0, 1))
    lane = iota((96, LANES), 1)
    for clip in range(CLIPS):
        y = dconv[clip * 96 : (clip + 1) * 96]
        total = taps_ref[:, 0:1] * y
        for step in range(1, TAPS):
            moved = pltpu.roll(y, 512 - step, 1)
            end = jnp.where(lane < LANES - step, moved[:, 384:], 0.0)
            total = total + taps_ref[:, step : step + 1] * jnp.concatenate([moved[:, :384], end], 1)
        back_ref[pl.ds(clip * 96, 96), :] = total


def get_columns(place_ref, in_refs, first_ref):
    for zh, in_ref in enumerate(in_refs):
        rest = in_ref[:, pl.ds(112, 8), :].astype(F32)
        begin = iota(rest.shape, 2) < 64
        low = jnp.where(begin, rest, 0.0)
        high = jnp.where(begin, pltpu.roll(rest, 64, 2), 0.0)
        last = jnp.concatenate([low, high], 1).astype(BF16)
        for block in range(8):
            source = owner(place_ref, 4 - block // 2, 4 - zh, 2 - block % 2)
            for tile in range(7):
                first_ref[source, :, tile * LANES : (tile + 1) * LANES] = in_ref[block, pl.ds(tile * 16, 16), :]
            first_ref[source, :, 7 * LANES :] = last[block]


def right_kernel(place_ref, in0_ref, in1_ref, in2_ref, in3_ref, front_ref, rear_ref, part_ref, first_ref):
    get_columns(place_ref, (in0_ref, in1_ref, in2_ref, in3_ref), first_ref)
    for at in range(0, 512, 128):
        rows = first_ref[pl.ds(at // 16, 8)].reshape(128, 1024)
        full = dot(rows[:, :512], front_ref[...], (1, 0)) + dot(rows[:, 512:], rear_ref[...], (1, 0))
        kept = jnp.where(iota(full.shape, 1) // 32 == iota(full.shape, 0) % 16, full, 0.0)
        total = jnp.sum(kept.reshape(8, 16, 512), 1)
        for tile in range(4):
            part_ref[pl.ds(at // 4 + tile, 8, stride=4), :] = total[:, tile * LANES : (tile + 1) * LANES]


def end_kernel(place_ref, in0_ref, in1_ref, in2_ref, in3_ref, wide_ref, frames_ref, grad_ref, back_ref, after_ref, taps_ref, mixed_ref, out_ref, first_ref):
    get_columns(place_ref, (in0_ref, in1_ref, in2_ref, in3_ref), first_ref)
    place = (iota((8, LANES), 1) == iota((8, LANES), 0)).astype(F32)
    lane = iota((96, LANES), 1)
    second = dot(first_ref[...].reshape(512, 1024), wide_ref[...], (0, 0))
    for clip in range(CLIPS):
        here = pl.ds(clip * 96, 96)
        x = frames_ref[here, :].astype(F32)
        cot = grad_ref[here, :].astype(F32)
        sig = jax.nn.sigmoid(x)
        sec = second[clip * 96 : (clip + 1) * 96]
        mixed_ref[here, :] = (sec * (x * sig)).astype(BF16)
        total = cot * sec * sig * (1.0 + x * (1.0 - sig)) + back_ref[here, :]
        after = dot(after_ref[:, clip * 96 : (clip + 1) * 96], place, (0, 0), HIGHEST)
        end = total[:, 384:]
        for step in range(1, TAPS):
            term = taps_ref[:, step : step + 1] * pltpu.roll(after, LANES - step, 1)
            end = end + jnp.where(lane >= LANES - step, term, 0.0)
        out_ref[here, :] = jnp.concatenate([total[:, :384], end], 1).astype(BF16)


def exchange(value, axes):
    return lax.all_to_all(value, axes, split_axis=0, concat_axis=0, tiled=True)


def along_seq(value, steps):
    pairs = [(s, s + steps) for s in range(32) if 0 <= s + steps < 32]
    return lax.ppermute(value, SEQ, pairs)


def ahead(value, axis, step):
    count = lax.axis_size(axis)
    return lax.ppermute(value, axis, [(s, (s + step) % count) for s in range(count)])


def gather_rows(near, far):
    shape = (4, 4, 120, LANES)
    near, far = near.reshape(shape), ahead(far, "c", 1).reshape(shape)
    both = [jnp.stack([near[step], far[step]]) for step in range(4)]
    both = [both[0]] + [ahead(both[step], "y", step) for step in range(1, 4)]
    return [jnp.stack([part[:, step] for part in both]).reshape(8, 120, LANES) for step in range(4)]


def halves_met(part, axis, apart, along):
    size = part.shape[along] // 2
    upper = lax.axis_index(axis) // apart % 2
    mine = lax.dynamic_slice_in_dim(part, upper * size, size, along)
    other = lax.dynamic_slice_in_dim(part, (1 - upper) * size, size, along)
    return mine, lax.ppermute(other, axis, [(s, s ^ apart) for s in range(lax.axis_size(axis))])


def total_kernel(in_ref, out_ref):
    total = jnp.sum(in_ref[...], 0)
    for row in range(8):
        for group in range(4):
            piece = total[row : row + 1, group * 32 : group * 32 + 32]
            out_ref[row % 4 * 4 + group, row // 4 : row // 4 + 1, :] = piece


def shards(frames, conv_taps, left_factor, right_factor, out_grad):
    x = frames.reshape(960, 512)
    cot = out_grad.reshape(960, 512)
    left = left_factor.reshape(512, 512)
    taps = conv_taps.T
    blocks = ((32, 120, LANES), BF16)

    (edge,) = call(edge_kernel, [((16, 960), BF16)])(x)
    edge = along_seq(edge, 1)
    right = right_factor.reshape(512, 32)
    (sent_back,) = call(back_kernel, [blocks])(x, cot, right)
    sent_back, edge = lax.optimization_barrier((sent_back, edge))
    back = exchange(sent_back, SEQ)
    place = jnp.stack([lax.axis_index(axis) for axis in SEQ]).astype(jnp.int32)
    part = ((16, 120, LANES), BF16)
    conv, near, far = call(
        conv_kernel,
        [((1024, 512), BF16), part, part],
        scratch=[pltpu.VMEM((32, 16, 512), F32)] * 2,
        scalars=1,
        arrays=4,
    )(place, x, edge, taps, left)
    rows = gather_rows(near, far)
    columns = [rows[0]] + [ahead(rows[step], "zh", step) for step in range(1, 4)]

    left_part, dfirst, dedge = call(left_kernel, [((512, 512), F32), ((512, 1024), BF16), ((8, 1024), F32)])(
        back, conv, left
    )
    after = along_seq(dedge, -1)
    (conv_back,) = call(dconv_kernel, [((960, 512), F32)], flops=1 << 35)(dfirst, taps, left)
    left_sum = jnp.sum(exchange(left_part.reshape(4, 128, 512), "x"), 0)
    left_sum = lax.optimization_barrier((left_sum, conv_back))[0]
    kept, met = halves_met(left_sum.reshape(2, 2, 32, 512), "zl", 1, 1)
    late = lax.optimization_barrier((x, cot, right, dedge))
    (wide,) = call(wide_kernel, [((512, 512), BF16)], flops=1 << 31)(late[2])
    (front,) = call(front_gate_kernel, [((512, 512), BF16)], flops=1 << 31)(*late[:2])
    (rear,) = call(rear_gate_kernel, [((512, 512), BF16)], flops=1 << 31)(*late[:2])
    columns, after, conv_back, front, rear, wide = lax.optimization_barrier(
        (columns, after, conv_back, front, rear, wide)
    )

    scratch = [pltpu.VMEM((32, 16, 1024), BF16)]
    (right_part,) = call(right_kernel, [((128, LANES), F32)], scratch=scratch, scalars=1, arrays=6)(
        place, *columns, front, rear
    )
    right_all = exchange(right_part.reshape(16, 8, LANES), CHAN)
    met = lax.optimization_barrier((met, right_part))[0]
    left_grad = sum(halves_met(kept + met, "zl", 2, 0))
    mixed, frames_grad = call(
        end_kernel, [((960, 512), BF16), ((960, 512), BF16)], scratch=scratch, scalars=1, arrays=10
    )(place, *columns, wide, x, cot, conv_back, after, taps)
    (right_grad,) = call(total_kernel, [((16, 2, 32), F32)])(right_all)
    return (
        mixed.reshape(frames.shape),
        frames_grad.reshape(frames.shape),
        left_grad.reshape(1, 32, 512),
        right_grad,
    )


def solution(mesh):
    fine = Mesh(mesh.devices.reshape(4, 4, 2, 4, 4), SEQ + CHAN)
    placed = (
        P(None, CHAN, SEQ),
        P(None, CHAN),
        P(SEQ, None, None),
        P(SEQ, None, None),
        P(None, CHAN, SEQ),
    )
    return jax.shard_map(
        shards,
        mesh=fine,
        in_specs=placed,
        out_specs=(
            P(None, CHAN, SEQ),
            P(None, CHAN, SEQ),
            P(SEQ, CHAN, None),
            P(SEQ, CHAN, None),
        ),
        check_vma=False,
    )
```

```python
import jax
import jax.numpy as jnp
from jax import lax
from jax.experimental import pallas as pl
from jax.experimental.pallas import tpu as pltpu
from jax.sharding import Mesh
from jax.sharding import PartitionSpec as P

TAPS = 4
CLIPS = 10
LANES = 128
SEQ = ("y", "zh", "c")
CHAN = ("x", "zl")
F32 = jnp.float32
BF16 = jnp.bfloat16
HIGHEST = lax.Precision.HIGHEST
LIMIT = pltpu.CompilerParams(vmem_limit_bytes=24 * 1024 * 1024)


def dot(left, right, sides, precision=None):
    return lax.dot_general(
        left,
        right,
        (((sides[0],), (sides[1],)), ((), ())),
        precision=precision,
        preferred_element_type=F32,
    )


def iota(shape, axis):
    return lax.broadcasted_iota(jnp.int32, shape, axis)


def call(kernel, outs, scratch=(), flops=1 << 29, moved=1 << 22, scalars=0, arrays=0):
    specs = {}
    if scalars:
        specs["in_specs"] = [pl.BlockSpec(memory_space=pltpu.SMEM)] * scalars + [
            pl.BlockSpec(memory_space=pltpu.VMEM)
        ] * arrays
    return pl.pallas_call(
        kernel,
        **specs,
        out_shape=[jax.ShapeDtypeStruct(shape, dtype) for shape, dtype in outs],
        scratch_shapes=list(scratch),
        compiler_params=LIMIT,
        cost_estimate=pl.CostEstimate(flops=flops, bytes_accessed=moved, transcendentals=0),
    )


def put_blocks(out_refs, at, rows, piece):
    blocks = piece.astype(BF16).reshape(32, rows, LANES)
    each = 32 // len(out_refs)
    for part, out_ref in enumerate(out_refs):
        out_ref[:, pl.ds(at, rows), :] = blocks[part * each : (part + 1) * each]


def put_tiles(out_refs, at, value):
    for tile in range(value.shape[1] // LANES):
        put_blocks(out_refs, (at + tile) * 16, 16, value[:, tile * LANES : (tile + 1) * LANES])


def halves(matrix):
    parts = matrix.reshape(32, 16, matrix.shape[1])
    return [parts[:, low : low + 8].reshape(256, -1).astype(BF16) for low in (0, 8)]


def put_rest(out_refs, matrix, rest):
    low, high = halves(matrix)
    none = jnp.zeros_like(rest)
    packed = dot(low, jnp.concatenate([rest, none], 0), (1, 1)) + dot(
        high, jnp.concatenate([none, rest], 0), (1, 1)
    )
    put_blocks(out_refs, 112, 8, packed)


def get_tiles(in_ref, held_ref):
    for tile in range(7):
        held_ref[:, tile * LANES : (tile + 1) * LANES] = in_ref[:, pl.ds(tile * 16, 16), :].reshape(512, LANES)
    rest = in_ref[:, pl.ds(112, 8), :].astype(F32)
    first = iota(rest.shape, 2) < 64
    low = jnp.where(first, rest, 0.0)
    high = jnp.where(first, pltpu.roll(rest, 64, 2), 0.0)
    whole = jnp.concatenate([low, high], 1).reshape(512, LANES)
    held_ref[:, 7 * LANES :] = whole.astype(BF16)


def owner(place_ref, y, zh, c):
    return (
        lax.rem(place_ref[0] + y, 4) * 8 + lax.rem(place_ref[1] + zh, 4) * 2 + lax.rem(place_ref[2] + c, 2)
    )


def edge_kernel(frames_ref, edge_ref):
    pick = (iota((16, LANES), 1) == iota((16, LANES), 0) + 112).astype(BF16)
    edge_ref[...] = dot(pick, frames_ref[:, 384:], (1, 1)).astype(BF16)


def widened(right_ref):
    row, column = iota((512, 512), 0), iota((512, 512), 1)
    order = (column == (row % 16) * 32 + row // 16).astype(BF16)
    repeat = (iota((32, 512), 0) == iota((32, 512), 1) % 32).astype(BF16)
    tall = dot(order, right_ref[...], (1, 0)).astype(BF16)
    return jnp.where(column // 32 == row % 16, dot(tall, repeat, (1, 0)), 0.0)


def gated(frames_ref, grad_ref, here):
    x = frames_ref[here, :].astype(F32)
    cot = grad_ref[here, :].astype(F32)
    return (cot * (x * jax.nn.sigmoid(x))).astype(BF16)


def back_kernel(frames_ref, grad_ref, right_ref, out_ref):
    wide = widened(right_ref)
    narrow = wide.astype(BF16)
    for at in range(0, 960, 256):
        rows = min(256, 960 - at)
        dsecond = gated(frames_ref, grad_ref, pl.ds(at, rows))
        whole = rows // LANES * LANES
        put_tiles([out_ref], at // LANES, dot(narrow, dsecond[:whole], (1, 1)))
        if rows > whole:
            put_rest([out_ref], wide, dsecond[whole:])


def wide_kernel(right_ref, wide_ref):
    wide_ref[...] = widened(right_ref).astype(BF16)


def front_gate_kernel(frames_ref, grad_ref, dsecond_ref):
    for at in range(0, 512, 128):
        dsecond_ref[pl.ds(at, 128), :] = gated(frames_ref, grad_ref, pl.ds(at, 128))


def rear_gate_kernel(frames_ref, grad_ref, dsecond_ref):
    for at in range(0, 448, 64):
        dsecond_ref[pl.ds(at, 64), :] = gated(frames_ref, grad_ref, pl.ds(512 + at, 64))
    dsecond_ref[448:, :] = jnp.zeros((64, 512), BF16)


def conv_kernel(place_ref, frames_ref, edge_ref, taps_ref, left_ref, conv_ref, near_ref, far_ref, turned_ref, order_ref):
    place = (iota((16, LANES), 1) == iota((16, LANES), 0) + 112).astype(BF16)
    lane = iota((96, LANES), 1)
    for clip in range(CLIPS):
        here = pl.ds(clip * 96, 96)
        x = frames_ref[here, :].astype(F32)
        before = dot(edge_ref[:, clip * 96 : (clip + 1) * 96], place, (0, 0))
        total = taps_ref[:, 0:1] * x
        for step in range(1, TAPS):
            moved = pltpu.roll(x, step, 1)
            start = jnp.where(lane < step, pltpu.roll(before, step, 1), moved[:, :LANES])
            total = total + taps_ref[:, step : step + 1] * jnp.concatenate([start, moved[:, LANES:]], 1)
        conv_ref[here, :] = total.astype(BF16)
    conv_ref[960:, :] = jnp.zeros((64, 512), BF16)
    turned_ref[...] = left_ref[...].astype(F32).T.reshape(32, 16, 512)
    for block in range(32):
        order_ref[block] = turned_ref[owner(place_ref, block // 4 % 4, block % 4, block // 16)]
    turned = order_ref[...].reshape(512, 512)
    narrow = turned.astype(BF16)
    for at in range(0, 960, 256):
        rows = min(256, 960 - at)
        whole = rows // LANES * LANES
        conv = conv_ref[pl.ds(at, rows), :]
        put_tiles([near_ref, far_ref], at // LANES, dot(narrow, conv[:whole], (1, 1)))
        if rows > whole:
            put_rest([near_ref, far_ref], turned, conv[whole:])


def left_kernel(in_ref, conv_ref, left_ref, part_ref, dfirst_ref, edge_ref):
    get_tiles(in_ref, dfirst_ref)
    edge_ref[...] = dot(left_ref[0:16, :], dfirst_ref[...], (1, 0))[0:8]
    part_ref[...] = dot(conv_ref[...], dfirst_ref[...], (0, 1))


def dconv_kernel(dfirst_ref, taps_ref, left_ref, back_ref):
    dconv = dot(dfirst_ref[...], left_ref[...], (0, 1))
    lane = iota((96, LANES), 1)
    for clip in range(CLIPS):
        y = dconv[clip * 96 : (clip + 1) * 96]
        total = taps_ref[:, 0:1] * y
        for step in range(1, TAPS):
            moved = pltpu.roll(y, 512 - step, 1)
            end = jnp.where(lane < LANES - step, moved[:, 384:], 0.0)
            total = total + taps_ref[:, step : step + 1] * jnp.concatenate([moved[:, :384], end], 1)
        back_ref[pl.ds(clip * 96, 96), :] = total


def get_columns(place_ref, in_refs, first_ref):
    for zh, in_ref in enumerate(in_refs):
        rest = in_ref[:, pl.ds(112, 8), :].astype(F32)
        begin = iota(rest.shape, 2) < 64
        low = jnp.where(begin, rest, 0.0)
        high = jnp.where(begin, pltpu.roll(rest, 64, 2), 0.0)
        last = jnp.concatenate([low, high], 1).astype(BF16)
        for block in range(8):
            source = owner(place_ref, 4 - block // 2, 4 - zh, 2 - block % 2)
            for tile in range(7):
                first_ref[source, :, tile * LANES : (tile + 1) * LANES] = in_ref[block, pl.ds(tile * 16, 16), :]
            first_ref[source, :, 7 * LANES :] = last[block]


def right_kernel(place_ref, in0_ref, in1_ref, in2_ref, in3_ref, front_ref, rear_ref, part_ref, first_ref):
    get_columns(place_ref, (in0_ref, in1_ref, in2_ref, in3_ref), first_ref)
    for at in range(0, 512, 128):
        rows = first_ref[pl.ds(at // 16, 8)].reshape(128, 1024)
        full = dot(rows[:, :512], front_ref[...], (1, 0)) + dot(rows[:, 512:], rear_ref[...], (1, 0))
        kept = jnp.where(iota(full.shape, 1) // 32 == iota(full.shape, 0) % 16, full, 0.0)
        total = jnp.sum(kept.reshape(8, 16, 512), 1)
        for tile in range(4):
            part_ref[pl.ds(at // 4 + tile, 8, stride=4), :] = total[:, tile * LANES : (tile + 1) * LANES]


def end_kernel(place_ref, in0_ref, in1_ref, in2_ref, in3_ref, wide_ref, frames_ref, grad_ref, back_ref, after_ref, taps_ref, mixed_ref, out_ref, first_ref):
    get_columns(place_ref, (in0_ref, in1_ref, in2_ref, in3_ref), first_ref)
    place = (iota((8, LANES), 1) == iota((8, LANES), 0)).astype(F32)
    lane = iota((96, LANES), 1)
    second = dot(first_ref[...].reshape(512, 1024), wide_ref[...], (0, 0))
    for clip in range(CLIPS):
        here = pl.ds(clip * 96, 96)
        x = frames_ref[here, :].astype(F32)
        cot = grad_ref[here, :].astype(F32)
        sig = jax.nn.sigmoid(x)
        sec = second[clip * 96 : (clip + 1) * 96]
        mixed_ref[here, :] = (sec * (x * sig)).astype(BF16)
        total = cot * sec * sig * (1.0 + x * (1.0 - sig)) + back_ref[here, :]
        after = dot(after_ref[:, clip * 96 : (clip + 1) * 96], place, (0, 0), HIGHEST)
        end = total[:, 384:]
        for step in range(1, TAPS):
            term = taps_ref[:, step : step + 1] * pltpu.roll(after, LANES - step, 1)
            end = end + jnp.where(lane >= LANES - step, term, 0.0)
        out_ref[here, :] = jnp.concatenate([total[:, :384], end], 1).astype(BF16)


def exchange(value, axes):
    return lax.all_to_all(value, axes, split_axis=0, concat_axis=0, tiled=True)


def along_seq(value, steps):
    pairs = [(s, s + steps) for s in range(32) if 0 <= s + steps < 32]
    return lax.ppermute(value, SEQ, pairs)


def ahead(value, axis, step):
    count = lax.axis_size(axis)
    return lax.ppermute(value, axis, [(s, (s + step) % count) for s in range(count)])


def gather_rows(near, far):
    shape = (4, 4, 120, LANES)
    near, far = near.reshape(shape), ahead(far, "c", 1).reshape(shape)
    both = [jnp.stack([near[step], far[step]]) for step in range(4)]
    both = [both[0]] + [ahead(both[step], "y", step) for step in range(1, 4)]
    return [jnp.stack([part[:, step] for part in both]).reshape(8, 120, LANES) for step in range(4)]


def halves_met(part, axis, apart, along, sent=F32):
    size = part.shape[along] // 2
    upper = lax.axis_index(axis) // apart % 2
    mine = lax.dynamic_slice_in_dim(part, upper * size, size, along)
    other = lax.dynamic_slice_in_dim(part, (1 - upper) * size, size, along)
    return mine, lax.ppermute(other.astype(sent), axis, [(s, s ^ apart) for s in range(lax.axis_size(axis))])


def total_kernel(in_ref, out_ref):
    total = jnp.sum(in_ref[...], 0)
    for row in range(8):
        for group in range(4):
            piece = total[row : row + 1, group * 32 : group * 32 + 32]
            out_ref[row % 4 * 4 + group, row // 4 : row // 4 + 1, :] = piece


def shards(frames, conv_taps, left_factor, right_factor, out_grad):
    x = frames.reshape(960, 512)
    cot = out_grad.reshape(960, 512)
    left = left_factor.reshape(512, 512)
    taps = conv_taps.T
    blocks = ((32, 120, LANES), BF16)

    (edge,) = call(edge_kernel, [((16, 960), BF16)])(x)
    edge = along_seq(edge, 1)
    right = right_factor.reshape(512, 32)
    (sent_back,) = call(back_kernel, [blocks])(x, cot, right)
    sent_back, edge = lax.optimization_barrier((sent_back, edge))
    back = exchange(sent_back, SEQ)
    place = jnp.stack([lax.axis_index(axis) for axis in SEQ]).astype(jnp.int32)
    part = ((16, 120, LANES), BF16)
    conv, near, far = call(
        conv_kernel,
        [((1024, 512), BF16), part, part],
        scratch=[pltpu.VMEM((32, 16, 512), F32)] * 2,
        scalars=1,
        arrays=4,
    )(place, x, edge, taps, left)
    rows = gather_rows(near, far)
    columns = [rows[0]] + [ahead(rows[step], "zh", step) for step in range(1, 4)]

    left_part, dfirst, dedge = call(left_kernel, [((512, 512), F32), ((512, 1024), BF16), ((8, 1024), F32)])(
        back, conv, left
    )
    after = along_seq(dedge, -1)
    (conv_back,) = call(dconv_kernel, [((960, 512), F32)], flops=1 << 35)(dfirst, taps, left)
    left_sum = jnp.sum(exchange(left_part.reshape(4, 128, 512), "x"), 0)
    left_sum = lax.optimization_barrier((left_sum, conv_back))[0]
    kept, met = halves_met(left_sum.reshape(2, 2, 32, 512), "zl", 1, 1, BF16)
    late = lax.optimization_barrier((x, cot, right, dedge))
    (wide,) = call(wide_kernel, [((512, 512), BF16)], flops=1 << 31)(late[2])
    (front,) = call(front_gate_kernel, [((512, 512), BF16)], flops=1 << 31)(*late[:2])
    (rear,) = call(rear_gate_kernel, [((512, 512), BF16)], flops=1 << 31)(*late[:2])
    columns, after, conv_back, front, rear, wide = lax.optimization_barrier(
        (columns, after, conv_back, front, rear, wide)
    )

    scratch = [pltpu.VMEM((32, 16, 1024), BF16)]
    (right_part,) = call(right_kernel, [((128, LANES), F32)], scratch=scratch, scalars=1, arrays=6)(
        place, *columns, front, rear
    )
    right_all = exchange(right_part.reshape(16, 8, LANES), CHAN)
    met = lax.optimization_barrier((met, right_part))[0]
    left_grad = sum(halves_met(kept + met, "zl", 2, 0))
    mixed, frames_grad = call(
        end_kernel, [((960, 512), BF16), ((960, 512), BF16)], scratch=scratch, scalars=1, arrays=10
    )(place, *columns, wide, x, cot, conv_back, after, taps)
    (right_grad,) = call(total_kernel, [((16, 2, 32), F32)])(right_all)
    return (
        mixed.reshape(frames.shape),
        frames_grad.reshape(frames.shape),
        left_grad.reshape(1, 32, 512),
        right_grad,
    )


def solution(mesh):
    fine = Mesh(mesh.devices.reshape(4, 4, 2, 4, 4), SEQ + CHAN)
    placed = (
        P(None, CHAN, SEQ),
        P(None, CHAN),
        P(SEQ, None, None),
        P(SEQ, None, None),
        P(None, CHAN, SEQ),
    )
    return jax.shard_map(
        shards,
        mesh=fine,
        in_specs=placed,
        out_specs=(
            P(None, CHAN, SEQ),
            P(None, CHAN, SEQ),
            P(SEQ, CHAN, None),
            P(SEQ, CHAN, None),
        ),
        check_vma=False,
    )
```
